256 devices in a mesh: grp: 8 (over z_lo, core), dev: 32 (over x, z_hi, y).
Axes of the slice: x: 4, y: 4, z: 8 (z_hi: 2, z_lo: 4; z = z_hi * 4 + z_lo), core: 2. Of those that a mesh axis runs over, the one named last changes fastest.
Arguments:
- density: float32 [2, 8192, 8192], P(None, 'dev', 'grp'), may hold values from -64 to 64, as said below
- costate: float32 [2, 8192, 8192], P(None, 'dev', 'grp'), may hold values from -64 to 64, as said below
- phases: float32 [24, 2, 64], replicated, may hold values from -3.140625 to 3.140625
- displacements: float32 [24, 2, 2, 64, 64], replicated, may hold values from -0.5 to 0.5
- table_slot: int32 [24], replicated, may hold values from 0 to 23, each once
- checkpoint: int32 [1], replicated, may hold values from 0 to 22
Outputs:
- costate_start: float32 [2, 8192, 8192], P(None, 'dev', 'grp')
- phase_grads: float32 [2, 2, 64], replicated
The draws below stay inside these ranges and needn't reach their ends.
Inputs may be any that keep to these rules, and one draw needn't show every extreme that they name: `density`: Hermitian: real part symmetric, imaginary part antisymmetric. `costate`: Hermitian: real part symmetric, imaginary part antisymmetric. `table_slot`: every row of phases once.
All inputs are finite; a program needn't handle non-finite values.
Results may differ from the reference program's by a relative error of at most 0.00011.
Values sent between devices are 32-bit elements; how exact they have to be, the bound alone decides.
A program may use at most 128 MiB of HBM per device.

```python
import jax
import jax.numpy as jnp
from jax import lax

LEVELS = 64
TRANSMON = 2
TABLES = 24
WINDOW = 2
NN = 8192


def hermitian_pair(key):
    first_key, second_key = jax.random.split(key, 2)
    real_part = jax.random.normal(first_key, (NN, NN), jnp.float32)
    imag_part = jax.random.normal(second_key, (NN, NN), jnp.float32)
    real_part = (real_part + real_part.T) * 0.7071
    imag_part = (imag_part - imag_part.T) * 0.7071
    return jnp.stack([real_part, imag_part])


def draw_density(key, part):
    key = jax.random.fold_in(key, 11)
    pair = hermitian_pair(key)
    return pair


def draw_costate(key, part):
    key = jax.random.fold_in(key, 23)
    pair = hermitian_pair(key)
    return pair


def centred(key, extent, deviation, bound, held_as=jnp.bfloat16):
    array = jax.random.normal(key, extent, jnp.float32) * deviation
    return jnp.minimum(jnp.maximum(array, -bound), bound).astype(held_as)


def setup_inputs(seed: int = 0) -> dict:
    key_list = jax.random.split(jax.random.key(seed), 7)
    return {
        "density": draw_density(jax.random.fold_in(key_list[6], 71), 0),
        "costate": draw_costate(jax.random.fold_in(key_list[6], 71), 0),
        "phases": jnp.clip(jax.random.uniform(key_list[2], (TABLES, 2, LEVELS), jnp.float32, -3.140625, 3.140625), -3.140625, 3.140625),
        "displacements": centred(key_list[3], (TABLES, 2, 2, LEVELS, LEVELS), (2 * LEVELS) ** -0.5, 0.5, jnp.float32),
        "table_slot": jax.random.permutation(key_list[4], TABLES).astype(jnp.int32),
        "checkpoint": jax.random.randint(key_list[5], (1,), 0, TABLES - 1).astype(jnp.int32),
    }


HIGH = lax.Precision.HIGHEST


def quad(real_part, imag_part):
    return jnp.stack([jnp.stack([real_part, -imag_part]), jnp.stack([imag_part, real_part])])


def mode_apply(quads, field, dim):
    letters = "abcdef"
    source = "p" + letters[:dim - 1] + "m" + letters[dim:]
    target = "o" + letters[:dim - 1] + "n" + letters[dim:]
    return jnp.einsum("opnm," + source + "->" + target, quads, field, precision=HIGH)


def turn(field, rows_angle, cols_angle):
    angles = rows_angle[:, :, None, None, None, None] - cols_angle[None, None, None, :, :, None]
    cosine = jnp.cos(angles)
    sine = jnp.sin(angles)
    return jnp.stack([cosine * field[0] - sine * field[1], sine * field[0] + cosine * field[1]])


def both_sides(field, matrix, row_dim, forward):
    real_part = matrix[0]
    imag_part = matrix[1]
    if forward:
        left_side = quad(real_part, imag_part)
        right_side = quad(real_part, -imag_part)
    else:
        left_side = quad(real_part.T, -imag_part.T)
        right_side = quad(real_part.T, imag_part.T)
    return mode_apply(right_side, mode_apply(left_side, field, row_dim), row_dim + 3)


def grad_terms(snapped, pulled):
    return 2.0 * jnp.sum(snapped[0] * pulled[1] - snapped[1] * pulled[0], axis=(3, 4, 5))


def reference(density, costate, phases, displacements, table_slot, checkpoint):
    shaped = (2, LEVELS, LEVELS, TRANSMON, LEVELS, LEVELS, TRANSMON)
    state_zero = density.reshape(shaped)
    adjoint_two = costate.reshape(shaped)
    start = checkpoint[0]
    grids = []
    matrices = []
    for layer in range(WINDOW):
        slot = table_slot[start + layer]
        table = lax.dynamic_index_in_dim(phases, slot, 0, keepdims=False)
        grids.append(table[0][:, None] + table[1][None, :])
        matrices.append(lax.dynamic_index_in_dim(displacements, start + layer, 0, keepdims=False))
    snapped_zero = turn(state_zero, grids[0], grids[0])
    state_one = both_sides(both_sides(snapped_zero, matrices[0][1], 2, True), matrices[0][0], 1, True)
    snapped_one = turn(state_one, grids[1], grids[1])
    pulled_one = both_sides(both_sides(adjoint_two, matrices[1][1], 2, False), matrices[1][0], 1, False)
    adjoint_one = turn(pulled_one, -grids[1], -grids[1])
    pulled_zero = both_sides(both_sides(adjoint_one, matrices[0][0], 1, False), matrices[0][1], 2, False)
    adjoint_zero = turn(pulled_zero, -grids[0], -grids[0])
    stacked = []
    for terms in (grad_terms(snapped_zero, pulled_zero), grad_terms(snapped_one, pulled_one)):
        stacked.append(jnp.stack([jnp.sum(terms, axis=(1, 2)), jnp.sum(terms, axis=(0, 2))]))
    return adjoint_zero.reshape(2, NN, NN), jnp.stack(stacked)
```

```python
import functools

import jax
import jax.numpy as jnp
from jax import lax
from jax.experimental import pallas as pl
from jax.experimental.pallas import tpu as pltpu
from jax.sharding import PartitionSpec as P

LEVELS = 64
HIGH = lax.Precision.HIGH
HIGHEST = lax.Precision.HIGHEST


def place():
    g = lax.axis_index("grp")
    d = lax.axis_index("dev")
    return d // 8, (d // 4) % 2 * 4 + g // 2, d % 4, g % 2


def exchange_kernel(same, x_ref, o_ref, local_sem, send_sem, recv_sem):
    x, z, y, core = place()
    me = lax.axis_index("dev") * 8 + lax.axis_index("grp")
    own = pltpu.make_async_copy(x_ref.at[0] if same else x_ref.at[me], o_ref.at[me], local_sem)
    own.start()

    def body(step, carry):
        s = (step * 37) % 256
        tz = (z + s % 8) % 8
        tx = (x + s // 8 % 4) % 4
        ty = (y + s // 32 % 4) % 4
        tc = (core + s // 128) % 2
        td = tx * 8 + tz // 4 * 4 + ty
        tg = tz % 4 * 2 + tc
        pltpu.make_async_remote_copy(
            src_ref=x_ref.at[0] if same else x_ref.at[td * 8 + tg],
            dst_ref=o_ref.at[me],
            send_sem=send_sem,
            recv_sem=recv_sem,
            device_id=(tg, td),
            device_id_type=pl.DeviceIdType.MESH,
        ).start()
        return carry

    lax.fori_loop(1, 256, body, 0)
    own.wait()
    rest = o_ref.at[pl.ds(0, 255)]
    pltpu.make_async_copy(rest, rest, send_sem).wait()
    pltpu.make_async_copy(rest, rest, recv_sem).wait()


def exchange(x, same=False):
    return pl.pallas_call(
        functools.partial(exchange_kernel, same),
        out_shape=jax.ShapeDtypeStruct((256,) + x.shape[1:], x.dtype),
        in_specs=[pl.BlockSpec(memory_space=pltpu.VMEM)],
        out_specs=pl.BlockSpec(memory_space=pltpu.VMEM),
        scratch_shapes=[pltpu.SemaphoreType.DMA] * 3,
        compiler_params=pltpu.CompilerParams(has_side_effects=True, vmem_limit_bytes=40 * 2**20),
    )(x)


def cmul(spec, a, b, precision=HIGHEST):
    dot = functools.partial(jnp.einsum, spec, precision=precision)
    return jnp.stack([dot(a[0], b[0]) - dot(a[1], b[1]), dot(a[0], b[1]) + dot(a[1], b[0])])


def conj(a):
    return jnp.stack([a[0], -a[1]])


def phase_columns(matrix, angle):
    return cmul("ij,j->ij", matrix, jnp.stack([jnp.cos(angle), jnp.sin(angle)]))


def there(field):
    f = field.reshape(2, 2, 16, 8, 8, 16, 8)
    f = f.transpose(2, 5, 0, 1, 4, 3, 6).reshape(256, 16, 128)
    f = exchange(f).reshape(32, 8, 2, 2, 8, 64)
    return f.transpose(2, 0, 3, 1, 4, 5).reshape(2, 64, 64, 64)


def back(field):
    f = field.reshape(2, 32, 2, 8, 8, 64)
    f = f.transpose(1, 3, 0, 2, 4, 5).reshape(256, 16, 128)
    f = exchange(f).reshape(16, 16, 2, 2, 8, 8, 8)
    return f.transpose(2, 3, 0, 5, 4, 1, 6).reshape(2, 2, 128, 8, 128)


def per_device(density, costate, phases, displacements, table_slot, checkpoint):
    start = checkpoint[0]
    table = [phases[table_slot[start + l]] for l in range(2)]
    disp = [displacements[start + l] for l in range(2)]
    va, wa = [phase_columns(disp[l][0], table[l][0]) for l in range(2)]
    vb, wb = [phase_columns(disp[l][1], table[l][1]) for l in range(2)]
    ua = cmul("ij,jk->ik", wa, va)
    ub = cmul("ij,jk->ik", wb, vb)
    eye = jnp.eye(2, dtype=jnp.float32)
    ub2 = jnp.stack([jnp.kron(ub[0], eye), jnp.kron(ub[1], eye)])

    rho = density.reshape(2, 2, 128, 8, 128)
    c = there(costate)
    r = cmul("ij,ajbk->aibk", ub2, rho, HIGH)
    r = cmul("aibk,jk->aibj", r, conj(ub2), HIGH)
    r = there(r)
    q = cmul("nap,ab->nbp", c, ua, HIGH)
    y = back(cmul("nc,nap->cap", conj(ua), q, HIGH))
    f = cmul("nap,bap->nb", q, conj(r), HIGH)
    t = cmul("aibj,jk->aibk", y, ub2, HIGH)
    out = cmul("ki,akbj->aibj", conj(ub2), t, HIGH)
    jj = cmul("aibk,ajbk->ij", t, conj(rho), HIGH)
    jj = jj.reshape(2, 64, 2, 64, 2)
    jj = jj[:, :, 0, :, 0] + jj[:, :, 1, :, 1]

    def diag(a, b):
        return 2.0 * cmul("ij,ji->i", a, b)[1]

    def dagger(a):
        return conj(a.transpose(0, 2, 1))

    def grads(u, v, w, m):
        first = diag(dagger(u), m)
        second = diag(dagger(w), cmul("ij,jk->ik", m, dagger(v)))
        return jnp.stack([first, second])

    parts = jnp.stack([grads(ua, va, wa, f), grads(ub, vb, wb, jj)], axis=1)
    total = jnp.sum(exchange(parts.reshape(1, 2, 128), same=True), axis=0).reshape(2, 2, 64)
    return out.reshape(2, 256, 1024), total


def solution(mesh):
    return jax.shard_map(
        per_device,
        mesh=mesh,
        in_specs=(P(None, "dev", "grp"), P(None, "dev", "grp"), P(), P(), P(), P()),
        out_specs=(P(None, "dev", "grp"), P()),
        check_vma=False,
    )
```

```python
import functools

import jax
import jax.numpy as jnp
from jax import lax
from jax.experimental import pallas as pl
from jax.experimental.pallas import tpu as pltpu
from jax.sharding import PartitionSpec as P

LEVELS = 64
TILES = 256
MESH = pl.DeviceIdType.MESH
HIGHEST = lax.Precision.HIGHEST
F32 = jnp.float32
BF16 = jnp.bfloat16
NN = ((1,), (0,))
NT = ((1,), (1,))


def dot(a, b, dims=NN, precision=None):
    return lax.dot_general(a, b, (dims, ((), ())), precision=precision, preferred_element_type=F32)


def split(x):
    high = x.astype(BF16)
    return high, (x - high.astype(F32)).astype(BF16)


def dot3(a, b, dims=NN):
    return dot(a[0], b[0], dims) + dot(a[0], b[1], dims) + dot(a[1], b[0], dims)


def roll(x, shift):
    return pltpu.roll(x, shift % 128, 1)


def lane(rows=8):
    return lax.broadcasted_iota(jnp.int32, (rows, 128), 1)


def skew_back(x, shift):
    x = roll(x, -shift)
    row = lax.broadcasted_iota(jnp.int32, x.shape, 0)
    for bit in (1, 2, 4):
        x = jnp.where(row & bit == 0, x, roll(x, -bit))
    return x


def skew(x, shift):
    return pltpu.roll(x, shift % 128, 1, stride=1, stride_axis=0)


def swap_bit(a, b, weight, low):
    return jnp.where(low, a, roll(b, weight)), jnp.where(low, roll(a, -weight), b)


def place():
    g = lax.axis_index("grp")
    d = lax.axis_index("dev")
    return d // 8, d // 4 % 2 * 4 + g // 2, d % 4, g % 2


def target(x, z, y, core):
    return z % 4 * 2 + core, x * 8 + z // 4 * 4 + y


def for_others(act):
    x, z, y, core = place()

    def one(tx, tz, ty, tc):
        g, d = target(tx, tz, ty, tc)
        act(g, d)

    for dz in range(1, 8):
        one(x, (z + dz) % 8, y, core)

    def body(k, carry):
        tx, ty, tc = (x + k % 4) % 4, (y + k // 4 % 4) % 4, (core + k // 16) % 2
        for dz in (0, 4, 1, 5, 2, 6, 3, 7):
            one(tx, (z + dz) % 8, ty, tc)
        return carry

    lax.fori_loop(1, 32, body, 0)


def tile(t):
    return pl.ds(pl.multiple_of(t * 8, 8), 8)


def send_all(send, recv, send_sem, recv_sem):
    me = lax.axis_index("dev") * 8 + lax.axis_index("grp")

    def act(g, d):
        pltpu.make_async_remote_copy(
            src_ref=send.at[tile(d * 8 + g)],
            dst_ref=recv.at[tile(me)],
            send_sem=send_sem,
            recv_sem=recv_sem,
            device_id=(g, d),
            device_id_type=MESH,
        ).start()

    for_others(act)
    recv[tile(me), :] = send[tile(me), :]


def wait_all(ref, sem):
    rest = ref.at[pl.ds(0, 8 * (TILES - 1))]
    pltpu.make_async_copy(rest, rest, sem).wait()


def columns(index, width=128):
    return pl.ds(pl.multiple_of(index * width, width), width)


def pack(field, send, half_diagonal):
    ln = lane()
    first, middle = ln == 0, ln == 64
    low64, low32, low16 = ln < 64, ln & 32 == 0, ln & 16 == 0

    def body(al, carry):
        for bo in range(8):
            v = []
            for a0 in range(2):
                part = []
                for rb in range(2):
                    rows = pl.ds(a0 * 128 + rb * 64 + bo * 8, 8)
                    part.append([skew_back(field[ri, rows, columns(al)], rb * 64 + bo * 8) for ri in range(2)])
                (re0, im0), (re1, im1) = part
                v0 = jnp.where(low64, re0, roll(im0, 64))
                v0 = v0 + jnp.where(first, -im1, jnp.where(middle, roll(re1, 64), 0.0))
                if half_diagonal:
                    v0 = jnp.where(first | middle, 0.5 * v0, v0)
                v1 = jnp.where(low64, re1, roll(im1, 64))
                v1 = jnp.where(first, roll(re0, 64), jnp.where(middle, im0, v1))
                v.append([v0, v1])
            u = [swap_bit(v[0][rb], v[1][rb], 32, low32) for rb in range(2)]
            for h1 in range(2):
                w = swap_bit(u[0][h1], u[1][h1], 16, low16)
                for h0 in range(2):
                    send[pl.ds((h1 * 2 + h0) * 512 + bo * 64 + al, 8, stride=8), :] = w[h0]
        return carry

    lax.fori_loop(0, 8, body, 0)


def unpack(recv, upper, lower):
    ln = lane()
    first, middle = ln == 0, ln == 64
    low64, low32, low16 = ln < 64, ln & 32 == 0, ln & 16 == 0
    inner = low64 & (ln > 0)

    def body(al, carry):
        for bo in range(8):
            t = [recv[pl.ds(h * 512 + bo * 64 + al, 8, stride=8), :] for h in range(4)]
            u = [swap_bit(t[h1 * 2], t[h1 * 2 + 1], 16, low16) for h1 in range(2)]
            v = [swap_bit(u[0][rb], u[1][rb], 32, low32) for rb in range(2)]
            (v00, v10), (v01, v11) = v
            r00, r10, r01, r11 = [roll(q, 64) for q in (v00, v10, v01, v11)]
            zero = jnp.zeros_like(v00)
            ups = [
                [
                    jnp.where(first, 0.5 * (v00 + v10), jnp.where(middle, r01, jnp.where(low64, v00, zero))),
                    jnp.where(first, 0.5 * (r00 - r10), jnp.where(middle, v01, jnp.where(low64, r00, zero))),
                ],
                [
                    jnp.where(first, 0.5 * (r00 + r10), jnp.where(middle, r11, jnp.where(low64, v01, zero))),
                    jnp.where(first, 0.5 * (v10 - v00), jnp.where(middle, -v11, jnp.where(low64, r01, zero))),
                ],
            ]
            downs = [
                [jnp.where(inner, v10, zero), jnp.where(inner, -r10, zero)],
                [jnp.where(inner, v11, zero), jnp.where(inner, -r11, zero)],
            ]
            for rb in range(2):
                base = rb * 64 + bo * 8
                for ri in range(2):
                    upper[ri, pl.ds(base, 8), columns(al)] = skew(ups[rb][ri], base)
                    lower[ri, pl.ds(base, 8), columns(al)] = skew(downs[rb][ri], base)
        return carry

    lax.fori_loop(0, 8, body, 0)


def sign(rows):
    return jnp.where(lane(rows) < 64, -1.0, 1.0).astype(F32)


def mode_one(src, dst, g3, conjugate):
    sgn = sign(64)
    if conjugate:
        sgn = -sgn

    def body(i, carry):
        base = pl.multiple_of(i * 256, 256)
        x = jnp.concatenate([src[pl.ds(base + k * 64, 64), :] for k in range(4)], axis=1)
        high, low = split(x)
        p = dot(g3[...], jnp.concatenate([high, low, high], axis=0))
        for k in range(4):
            q = p[:, k * 128 : k * 128 + 128]
            dst[pl.ds(base + k * 64, 64), :] = q[:64] + sgn * roll(q[64:], 64)
        return carry

    lax.fori_loop(0, 8, body, 0)


def flip(src, dst):
    low32 = lane() & 32 == 0

    def body(c, carry):
        for k in range(4):
            e = [src[pl.ds(k * 512 + c * 2 + bit, 8, stride=64), :] for bit in range(2)]
            o = swap_bit(e[0], e[1], 32, low32)
            for bit in range(2):
                dst[pl.ds(c * 64 + k * 16 + bit, 8, stride=2), :] = o[bit]
        return carry

    lax.fori_loop(0, 32, body, 0)


def gram(x_ref, y_ref, flag):
    sgn = sign(64) * (-flag)

    def body(i, acc):
        for k in range(2):
            base = pl.multiple_of(i * 128 + k * 64, 64)
            x = x_ref[pl.ds(base, 64), :]
            xh, xl = split(jnp.concatenate([x, sgn * roll(x, 64)], axis=0))
            yh, yl = split(y_ref[pl.ds(base, 64), :])
            acc = acc + dot(
                jnp.concatenate([xh, xh, xl, xl], axis=1), jnp.concatenate([yh, yl, yh, yl], axis=1), NT
            )
        return acc

    return lax.fori_loop(0, 16, body, jnp.zeros((128, 64), F32))


def cmul(a, b, dims=NN):
    mul = functools.partial(dot, dims=dims, precision=HIGHEST)
    return mul(a[0], b[0]) - mul(a[1], b[1]), mul(a[0], b[1]) + mul(a[1], b[0])


def conj(a):
    return a[0], -a[1]


def diagonals(u, v, w, m):
    t = cmul(m, conj(v), NT)
    first = jnp.sum(u[0] * m[1] - u[1] * m[0], axis=0, keepdims=True)
    second = jnp.sum(w[0] * t[1] - w[1] * t[0], axis=0, keepdims=True)
    return 2.0 * first, 2.0 * second


def kernel(
    density, costate, phases, displacements, slots, checkpoint, out, grads,
    cin, rin, work, lower, disp, table, send_c, recv_c, send_r, recv_r, send_a, send_b, recv_a, recv_b,
    t1, t2, t3, t4, g3, left_hi, left_lo, right_hi, right_lo, result, tile_ref, near, far,
    load, sem,
):
    loads = []
    for k in range(2):
        loads.append(pltpu.make_async_copy(costate.at[k], cin.at[k], load.at[k]))
    for k in range(2):
        loads.append(pltpu.make_async_copy(density.at[k], rin.at[k], load.at[2 + k]))
    loads.append(pltpu.make_async_copy(displacements, disp, load.at[4]))
    loads.append(pltpu.make_async_copy(phases, table, load.at[5]))
    for copy in loads:
        copy.start()
    barrier = pltpu.get_barrier_semaphore()
    for_others(
        lambda g, d: pl.semaphore_signal(barrier, inc=1, device_id=(g, d), device_id_type=MESH)
    )
    loads[0].wait()
    loads[1].wait()
    pack(cin, send_c, False)
    pl.semaphore_wait(barrier, TILES - 1)
    send_all(send_c, recv_c, sem.at[0], sem.at[1])

    loads[4].wait()
    loads[5].wait()
    start = checkpoint[0]
    first, second = [], []
    for layer in range(2):
        angle = table[slots[start + layer]]
        cosine, sine = jnp.cos(angle), jnp.sin(angle)
        for mode, held in ((0, first), (1, second)):
            re, im = disp[start + layer, mode, 0], disp[start + layer, mode, 1]
            c, s = cosine[mode : mode + 1], sine[mode : mode + 1]
            held.append((re * c - im * s, re * s + im * c))
    va, wa = first
    vb, wb = second
    ua, ub = cmul(wa, va), cmul(wb, vb)
    gh, gl = split(jnp.concatenate([ua[0].T, ua[1].T], axis=0))
    g3[...] = jnp.concatenate([gh, gh, gl], axis=1)
    spread = (
        lax.broadcasted_iota(jnp.int32, (128, 64), 0) // 2 == lax.broadcasted_iota(jnp.int32, (128, 64), 1)
    ).astype(F32)
    parity = (
        lax.broadcasted_iota(jnp.int32, (128, 128), 0) + lax.broadcasted_iota(jnp.int32, (128, 128), 1)
    ) % 2 == 0

    def both(m):
        wide = dot(dot(spread, m, NN, HIGHEST), spread, NT, HIGHEST)
        return jnp.where(parity, wide, 0.0)

    ub, vb, wb = [(both(m[0]), both(m[1])) for m in (ub, vb, wb)]
    left = jnp.concatenate([jnp.concatenate([ub[0], -ub[1]], axis=1), jnp.concatenate([ub[1], ub[0]], axis=1)], axis=0)
    right = jnp.concatenate([jnp.concatenate([ub[0], ub[1]], axis=1), jnp.concatenate([-ub[1], ub[0]], axis=1)], axis=0)
    for k, (m, high, low) in enumerate(((left, left_hi, left_lo), (right, right_hi, right_lo))):
        for turned in range(2):
            h, l = split(m.T if turned else m)
            high[turned], low[turned] = h, l

    loads[2].wait()
    loads[3].wait()

    def rho_body(i, carry):
        wide = columns(i, 256)
        for a0 in range(2):
            rows = pl.ds(a0 * 128, 128)
            x = [rin[ri, rows, wide] for ri in range(2)]
            t = []
            for k in range(2):
                piece = jnp.concatenate([q[:, k * 128 : k * 128 + 128] for q in x], axis=1)
                t.append(dot3(split(piece), (right_hi[1], right_lo[1])))
            t = jnp.concatenate(
                [jnp.concatenate([q[:, :128] for q in t], axis=1), jnp.concatenate([q[:, 128:] for q in t], axis=1)],
                axis=0,
            )
            y = dot3((left_hi[0], left_lo[0]), split(t))
            work[0, rows, wide] = y[:128]
            work[1, rows, wide] = y[128:]
        return carry

    lax.fori_loop(0, 4, rho_body, 0)
    pack(work, send_r, True)
    send_all(send_r, recv_r, sem.at[2], sem.at[3])

    wait_all(recv_c, sem.at[1])
    mode_one(recv_c, t2, g3, False)
    flip(t2, t1)
    mode_one(t1, t2, g3, True)
    flip(t2, t3)
    low32 = lane(64) & 32 == 0

    def blend(i, carry):
        rows = pl.ds(pl.multiple_of(i * 64, 64), 64)
        a, b = swap_bit(t3[rows, :], t2[rows, :], 32, low32)
        send_a[rows, :] = a
        send_b[rows, :] = b
        return carry

    lax.fori_loop(0, 32, blend, 0)
    send_all(send_a, recv_a, sem.at[4], sem.at[5])
    send_all(send_b, recv_b, sem.at[6], sem.at[7])

    flip(recv_c, t2)
    mode_one(t2, t3, g3, True)
    flip(t3, t2)
    wait_all(recv_r, sem.at[3])
    flip(recv_r, t4)
    f = gram(t1, t4, 1.0) + gram(t2, recv_r, -1.0)
    row0, row1 = diagonals(ua, va, wa, (f[:64], f[64:]))

    total = jnp.zeros((256, 256), F32)
    stores = []
    for a0, (recv, number) in enumerate(((recv_a, 5), (recv_b, 7))):
        wait_all(recv, sem.at[number])
        unpack(recv, work, lower)
        rows = pl.ds(a0 * 128, 128)

        def final_body(i, acc, a0=a0, rows=rows):
            wide = columns(i, 256)
            t = []
            for k in range(2):
                chunk = columns(i * 2 + k)
                piece = jnp.concatenate(
                    [work[ri, pl.ds(0, 128), chunk] + lower[ri, :, chunk].T for ri in range(2)], axis=1
                )
                t.append(dot3(split(piece), (right_hi[0], right_lo[0])))
            t = jnp.concatenate(
                [jnp.concatenate([q[:, :128] for q in t], axis=1), jnp.concatenate([q[:, 128:] for q in t], axis=1)],
                axis=0,
            )
            th, tl = split(t)
            y = dot3((left_hi[1], left_lo[1]), (th, tl))
            result[0, rows, wide] = y[:128]
            result[1, rows, wide] = y[128:]
            rh, rl = split(jnp.concatenate([rin[ri, rows, wide] for ri in range(2)], axis=0))
            return acc + dot3((th, tl), (rh, rl), NT) + dot(tl, rl, NT)

        total = lax.fori_loop(0, 4, final_body, total)
        for ri in range(2):
            copy = pltpu.make_async_copy(result.at[ri, rows], out.at[ri, rows], load.at[a0 * 2 + ri])
            copy.start()
            stores.append(copy)
    j = (total[:128, :128] + total[128:, 128:], total[128:, :128] - total[:128, 128:])
    row2, row3 = diagonals(ub, vb, wb, j)
    blank = jnp.zeros((1, 64), F32)
    tile_ref[0] = jnp.concatenate(
        [jnp.concatenate([row0, blank], axis=1), jnp.concatenate([row1, blank], axis=1), row2, row3,
         jnp.zeros((4, 128), F32)], axis=0)

    x, z, y, core = place()
    for half in range(2):
        slots_ref = (near, far)[half]
        for k in range(1, 16):
            if half == 0:
                to = target(x, (z + k // 2) % 8, y, (core + k % 2) % 2)
            else:
                to = target((x + k // 4) % 4, z, (y + k % 4) % 4, core)
            pltpu.make_async_remote_copy(
                src_ref=tile_ref.at[half], dst_ref=slots_ref.at[k - 1], send_sem=sem.at[8 + half],
                recv_sem=sem.at[10 + half], device_id=to, device_id_type=MESH,
            ).start()
        pltpu.make_async_copy(slots_ref, slots_ref, sem.at[10 + half]).wait()
        value = tile_ref[half]
        for k in range(15):
            value = value + slots_ref[k]
        tile_ref[half + 1] = value
    summed = tile_ref[2]
    modes = dot(summed, spread, NN, HIGHEST)
    for layer in range(2):
        grads[layer, 0:1, :] = summed[layer : layer + 1, :64]
        grads[layer, 1:2, :] = modes[2 + layer : 3 + layer, :]
    for half in range(2):
        pltpu.make_async_copy((near, far)[half], (near, far)[half], sem.at[8 + half]).wait()
    wait_all(send_c, sem.at[0])
    wait_all(send_r, sem.at[2])
    wait_all(send_a, sem.at[4])
    wait_all(send_b, sem.at[6])
    for copy in stores:
        copy.wait()


def per_device(density, costate, phases, displacements, table_slot, checkpoint):
    anywhere = pl.BlockSpec(memory_space=pl.ANY)
    smem = pl.BlockSpec(memory_space=pltpu.SMEM)
    tiles = pltpu.VMEM((8 * TILES, 128), F32)
    return pl.pallas_call(
        kernel,
        out_shape=(jax.ShapeDtypeStruct(costate.shape, F32), jax.ShapeDtypeStruct((2, 2, LEVELS), F32)),
        in_specs=[anywhere] * 4 + [smem] * 2,
        out_specs=(anywhere, pl.BlockSpec(memory_space=pltpu.VMEM)),
        scratch_shapes=[
            pltpu.VMEM((2, 256, 1024), F32),
            pltpu.VMEM((2, 256, 1024), F32),
            pltpu.VMEM((2, 256, 1024), F32),
            pltpu.VMEM((2, 128, 1024), F32),
            pltpu.VMEM(displacements.shape, F32),
            pltpu.VMEM(phases.shape, F32),
        ]
        + [tiles] * 8
        + [tiles] * 4
        + [pltpu.VMEM((128, 192), BF16)]
        + [pltpu.VMEM((2, 256, 256), BF16)] * 4
        + [
            pltpu.VMEM((2, 256, 1024), F32),
            pltpu.VMEM((3, 8, 128), F32),
            pltpu.VMEM((15, 8, 128), F32),
            pltpu.VMEM((15, 8, 128), F32),
            pltpu.SemaphoreType.DMA((6,)),
            pltpu.SemaphoreType.DMA((12,)),
        ],
        compiler_params=pltpu.CompilerParams(
            collective_id=0, has_side_effects=True, vmem_limit_bytes=48 * 2**20
        ),
    )(density, costate, phases, displacements, table_slot, checkpoint)


def solution(mesh):
    return jax.shard_map(
        per_device,
        mesh=mesh,
        in_specs=(P(None, "dev", "grp"), P(None, "dev", "grp"), P(), P(), P(), P()),
        out_specs=(P(None, "dev", "grp"), P()),
        check_vma=False,
    )
```

```python
import functools

import jax
import jax.numpy as jnp
from jax import lax
from jax.experimental import pallas as pl
from jax.experimental.pallas import tpu as pltpu
from jax.sharding import PartitionSpec as P

LEVELS = 64
TILES = 256
PITCH = 72
MESH = pl.DeviceIdType.MESH
HIGHEST = lax.Precision.HIGHEST
F32 = jnp.float32
BF16 = jnp.bfloat16
NN = ((1,), (0,))
NT = ((1,), (1,))


def dot(a, b, dims=NN, precision=None):
    return lax.dot_general(a, b, (dims, ((), ())), precision=precision, preferred_element_type=F32)


def split(x):
    high = x.astype(BF16)
    return high, (x - high.astype(F32)).astype(BF16)


def dot3(a, b, dims=NN):
    return dot(a[0], b[0], dims) + dot(a[0], b[1], dims) + dot(a[1], b[0], dims)


def roll(x, shift):
    return pltpu.roll(x, shift % 128, 1)


def lane(rows=8):
    return lax.broadcasted_iota(jnp.int32, (rows, 128), 1)


def swap_bit(a, b, weight, low):
    return jnp.where(low, a, roll(b, weight)), jnp.where(low, roll(a, -weight), b)


def place():
    g = lax.axis_index("grp")
    d = lax.axis_index("dev")
    return d >> 3, ((d >> 2) & 1) * 4 + (g >> 1), d & 3, g & 1


def target(x, z, y, core):
    return (z & 3) * 2 + core, x * 8 + (z >> 2) * 4 + y


def apart(a, b):
    e = (a - b) & 7
    return jnp.minimum(e, 8 - e)


def tile(t):
    return pl.ds(pl.multiple_of(t * 8, 8), 8)


def slot(d, g):
    return pl.ds(pl.multiple_of(d * PITCH + g * 8, 8), 8)


def for_others(act):
    x, z, y, core = place()

    def one(tx, dz, ty, tc):
        g, d = target(tx, (z + dz) & 7, ty, tc)
        act(g, d, dz, (tx + ty + tc) & 1)

    for dz in range(1, 8):
        one(x, dz, y, core)

    def body(k, carry):
        tx, ty, tc = (x + k) & 3, (y + (k >> 2)) & 3, (core + (k >> 4)) & 1
        for dz in (0, 4, 1, 5, 2, 6, 3, 7):
            one(tx, dz, ty, tc)
        return carry

    lax.fori_loop(1, 32, body, 0)


def send_all(send, recv, send_sem, recv_sem):
    me_g, me_d = lax.axis_index("grp"), lax.axis_index("dev")

    def act(g, d, dz, parity):
        pltpu.make_async_remote_copy(
            src_ref=send.at[tile(d * 8 + g)],
            dst_ref=recv.at[tile(me_d * 8 + me_g)],
            send_sem=send_sem,
            recv_sem=recv_sem,
            device_id=(g, d),
            device_id_type=MESH,
        ).start()

    for_others(act)
    recv[tile(me_d * 8 + me_g), :] = send[tile(me_d * 8 + me_g), :]


def send_near(send, recv, send_sem, recv_sem):
    x, z, y, core = place()
    me_g, me_d = lax.axis_index("grp"), lax.axis_index("dev")
    quad = me_d >> 2
    alone = quad == me_g
    after = (quad > me_g).astype(jnp.int32)
    other = core * 4 + x
    nearer = []
    for dz in range(8):
        own, far = min(dz, 8 - dz), apart(other, z + dz)
        nearer.append(jnp.where(far == own, 2, jnp.where(own < far, 1, 0)))

    def copy(order, g, d):
        return pltpu.make_async_remote_copy(
            src_ref=send[order].at[tile(d * 8 + g)],
            dst_ref=recv[order].at[slot(me_d, me_g)],
            send_sem=send_sem.at[order],
            recv_sem=recv_sem.at[order],
            device_id=(g, d),
            device_id_type=MESH,
        )

    def act(g, d, dz, parity):
        chosen = jnp.where(nearer[dz] == 2, parity ^ after, nearer[dz]) == 1

        @pl.when(alone | chosen)
        def _():
            copy(0, g, d).start()

        @pl.when(jnp.logical_not(alone) & chosen)
        def _():
            copy(1, g, d).start()

    for_others(act)
    for order in range(2):
        recv[order][slot(me_d, me_g), :] = send[order][tile(me_d * 8 + me_g), :]


def wait_tiles(ref, sem, count):
    rest = ref.at[pl.ds(0, 8 * count)]
    pltpu.make_async_copy(rest, rest, sem).wait()


def wait_near(recv, recv_sem):
    alone = lax.axis_index("dev") >> 2 == lax.axis_index("grp")
    wait_tiles(recv[0], recv_sem.at[0], 143)
    for flag, count in ((alone, 112), (jnp.logical_not(alone), 111)):

        @pl.when(flag)
        def _(count=count):
            wait_tiles(recv[1], recv_sem.at[1], count)


def wait_near_sent(send, send_sem):
    alone = lax.axis_index("dev") >> 2 == lax.axis_index("grp")

    @pl.when(alone)
    def _():
        wait_tiles(send[0], send_sem.at[0], 255)

    @pl.when(jnp.logical_not(alone))
    def _():
        wait_tiles(send[0], send_sem.at[0], 127)
        wait_tiles(send[1], send_sem.at[1], 127)


def columns(index, width=128):
    return pl.ds(pl.multiple_of(index * width, width), width)


def masks(bo):
    ln = lane()
    window = (ln >= 8 * bo) & (ln < 8 * bo + 64)
    diagonal = ((ln & 63) >= 8 * bo) & ((ln & 63) < 8 * bo + 8)
    return ln < 64, ln & 32 == 0, window, diagonal


def quarter(rows=8):
    return jnp.where(lane(rows) < 64, -1.0, 1.0).astype(F32)


def pack(field, send, half_diagonal):
    sgn = quarter()

    def body(al, carry):
        for bo in range(8):
            low64, low32, window, diagonal = masks(bo)
            v = [[], []]
            for a0 in range(2):
                folded = []
                for rb in range(2):
                    rows = pl.ds(a0 * 128 + rb * 64 + bo * 8, 8)
                    re, im = [field[ri, rows, columns(al)] for ri in range(2)]
                    a = jnp.where(low64, re, im)
                    b = roll(jnp.where(low64, im, re), 64)
                    keep = window if rb == 0 else jnp.logical_not(window)
                    folded.append(jnp.where(keep, a, b))
                    if rb == 0:
                        rest = jnp.where(window, b, a)
                k = folded[0] + sgn * roll(folded[1], 64)
                if half_diagonal:
                    k = 0.5 * k
                v[0].append(jnp.where(diagonal, k, folded[0]))
                v[1].append(jnp.where(diagonal, rest, folded[1]))
            for rb in range(2):
                w = swap_bit(v[rb][0], v[rb][1], 32, low32)
                for h in range(2):
                    send[pl.ds(h * 1024 + rb * 512 + bo * 64 + al, 8, stride=8), :] = w[h]
        return carry

    lax.fori_loop(0, 8, body, 0)


def turn_over(field, dst):
    def body(al, carry):
        for a0 in range(2):
            rows = pl.ds(a0 * 128, 128)
            dst[0, rows, columns(al)] = field[0, rows, columns(al)].T
            dst[1, rows, columns(al)] = -(field[1, rows, columns(al)].T)
        return carry

    lax.fori_loop(0, 8, body, 0)


def unpack(recv, upper, lower):
    sgn = quarter()

    def body(al, carry):
        for bo in range(8):
            low64, low32, window, diagonal = masks(bo)
            outside = diagonal & jnp.logical_not(low64)
            v = []
            for rb in range(2):
                t = [recv[pl.ds(h * 1024 + rb * 512 + bo * 64 + al, 8, stride=8), :] for h in range(2)]
                v.append(swap_bit(t[0], t[1], 32, low32))
            for order, dst in ((0, upper), (1, lower)):
                v0, v1 = v[0][order], v[1][order]
                if order == 1:
                    v0, v1 = -sgn * v0, -sgn * v1
                r0, r1 = roll(v0, 64), roll(v1, 64)
                way = -0.5 if order == 0 else 0.5
                u0, s0 = jnp.where(diagonal, 0.5 * v0, v0), jnp.where(diagonal, 0.5 * r0, r0)
                u1, s1 = jnp.where(diagonal, way * sgn * r0, v1), jnp.where(diagonal, -way * sgn * v0, r1)
                rows = pl.ds(bo * 8, 8)
                dst[0, rows, columns(al)] = jnp.where(window, jnp.where(low64, u0, s0), jnp.where(outside, r1, 0.0))
                dst[1, rows, columns(al)] = jnp.where(window, jnp.where(low64, s0, u0), jnp.where(outside, v1, 0.0))
                rows = pl.ds(64 + bo * 8, 8)
                dst[0, rows, columns(al)] = jnp.where(window, 0.0, jnp.where(low64, u1, s1))
                dst[1, rows, columns(al)] = jnp.where(window, 0.0, jnp.where(low64, s1, u1))
        return carry

    lax.fori_loop(0, 8, body, 0)


def mode_one(src, dst, g3, conjugate):
    sgn = quarter(64)
    if conjugate:
        sgn = -sgn

    def body(i, carry):
        base = pl.multiple_of(i * (8 * PITCH), 8)
        for j in range(2):
            rows = [pl.ds(base + (4 * j + k) * PITCH, 64) for k in range(4)]
            x = jnp.concatenate([src[r, :] for r in rows], axis=1)
            high, low = split(x)
            p = dot(g3[...], jnp.concatenate([high, low, high], axis=0))
            for k in range(4):
                q = p[:, k * 128 : k * 128 + 128]
                dst[rows[k], :] = q[:64] + sgn * roll(q[64:], 64)
        return carry

    lax.fori_loop(0, 4, body, 0)


def sent_direct(quad, k, alone):
    x, z, y, core = place()
    g = 2 * k + (lax.broadcasted_iota(jnp.int32, (8, 128), 0) >> 2)
    own = apart((quad & 1) * 4 + (g >> 1), z)
    far = apart((g & 1) * 4 + (quad >> 1), z)
    parity = (x + y + core) & 1
    tie = jnp.where(quad > g, 1, 0) != parity
    chosen = (own < far) | ((own == far) & tie)
    return (quad == g) | chosen if alone else (quad != g) & chosen


def flip(src, dst, direct=None, alone=True):
    low32 = lane() & 32 == 0

    def body(quad, carry):
        for k in range(4):
            if direct is not None:
                keep = sent_direct(quad, k, alone)
            for j in range(4):
                c = quad * 4 + j
                e = [src[pl.ds(k * (8 * PITCH) + c * 2 + bit, 8, stride=PITCH), :] for bit in range(2)]
                o = swap_bit(e[0], e[1], 32, low32)
                for bit in range(2):
                    rows = pl.ds(c * PITCH + k * 16 + bit, 8, stride=2)
                    value = o[bit]
                    if direct is not None:
                        value = jnp.where(keep, direct[rows, :], value)
                    dst[rows, :] = value
        return carry

    lax.fori_loop(0, 8, body, 0)


def blend(y1, y2, send_a, send_b):
    low32 = lane(64) & 32 == 0

    def body(i, carry):
        for k in range(4):
            c = i * 4 + k
            held = pl.ds(pl.multiple_of(c * PITCH, 8), 64)
            rows = pl.ds(pl.multiple_of(c * 64, 64), 64)
            send_a[rows, :], send_b[rows, :] = swap_bit(y1[held, :], y2[held, :], 32, low32)
        return carry

    lax.fori_loop(0, 8, body, 0)


def gram(x_ref, y_ref, flag):
    sgn = quarter(64) * (-flag)

    def body(i, acc):
        xs, ys = [], []
        for k in range(4):
            rows = pl.ds(pl.multiple_of(i * (4 * PITCH), 8) + k * PITCH, 64)
            x = x_ref[rows, :]
            xh, xl = split(jnp.concatenate([x, sgn * roll(x, 64)], axis=0))
            yh, yl = split(y_ref[rows, :])
            xs += [xh, xh, xl, xl]
            ys += [yh, yl, yh, yl]
        return acc + dot(jnp.concatenate(xs, axis=1), jnp.concatenate(ys, axis=1), NT)

    return lax.fori_loop(0, 8, body, jnp.zeros((128, 64), F32))


def cmul(a, b, dims=NN):
    mul = functools.partial(dot, dims=dims, precision=HIGHEST)
    return mul(a[0], b[0]) - mul(a[1], b[1]), mul(a[0], b[1]) + mul(a[1], b[0])


def conj(a):
    return a[0], -a[1]


def diagonals(u, v, w, m):
    t = cmul(m, conj(v), NT)
    first = jnp.sum(u[0] * m[1] - u[1] * m[0], axis=0, keepdims=True)
    second = jnp.sum(w[0] * t[1] - w[1] * t[0], axis=0, keepdims=True)
    return 2.0 * first, 2.0 * second


def across(x, right_hi, right_lo):
    t = []
    for k in range(2):
        piece = jnp.concatenate([q[:, k * 128 : k * 128 + 128] for q in x], axis=1)
        t.append(dot3(split(piece), (right_hi, right_lo)))
    return [jnp.concatenate([q[:, half * 128 : half * 128 + 128] for q in t], axis=1) for half in range(2)]


def rho_stage(rin, work, right_hi, right_lo, left_hi, left_lo):
    def body(i, carry):
        wide = columns(i, 256)
        t = across([rin[ri, :, wide] for ri in range(2)], right_hi[1], right_lo[1])
        for a0 in range(2):
            rows = pl.ds(a0 * 128, 128)
            y = dot3(
                (left_hi[0], left_lo[0]),
                split(jnp.concatenate([q[a0 * 128 : a0 * 128 + 128] for q in t], axis=0)),
            )
            work[0, rows, wide] = y[:128]
            work[1, rows, wide] = y[128:]
        return carry

    lax.fori_loop(0, 4, body, 0)


def final_stage(work, lower, rin, right_hi, right_lo, left_hi, left_lo, result, rows, total):
    def body(i, acc):
        wide = columns(i, 256)
        x = [
            jnp.concatenate(
                [work[ri, pl.ds(0, 128), columns(i * 2 + k)] + lower[ri, :, columns(i * 2 + k)].T for k in range(2)],
                axis=1,
            )
            for ri in range(2)
        ]
        th, tl = split(jnp.concatenate(across(x, right_hi[0], right_lo[0]), axis=0))
        y = dot3((left_hi[1], left_lo[1]), (th, tl))
        result[0, rows, wide] = y[:128]
        result[1, rows, wide] = y[128:]
        rh, rl = split(jnp.concatenate([rin[ri, rows, wide] for ri in range(2)], axis=0))
        return acc + dot3((th, tl), (rh, rl), NT) + dot(tl, rl, NT)

    return lax.fori_loop(0, 4, body, total)


def kernel(
    density, costate, phases, displacements, slots_hbm, checkpoint_hbm, out, grads,
    result, cin, rin, work, turned, lower, disp, table, slots, checkpoint,
    c_send0, c_send1, r_send0, r_send1, c_recv0, c_recv1, r_recv0, r_recv1, send_a, send_b, recv_a, recv_b,
    t1, t2, t3, t4, g3, left_hi, left_lo, right_hi, right_lo, tile_ref, near, far,
    ready, load, sem,
):
    c_send, r_send = (c_send0, c_send1), (r_send0, r_send1)
    c_recv, r_recv = (c_recv0, c_recv1), (r_recv0, r_recv1)
    x, z, y, core = place()
    loads = [
        pltpu.make_async_copy(costate.at[0], cin.at[0], load.at[0]),
        pltpu.make_async_copy(costate.at[1], cin.at[1], load.at[1]),
        pltpu.make_async_copy(density.at[0], rin.at[0], load.at[2]),
        pltpu.make_async_copy(density.at[1], rin.at[1], load.at[3]),
        pltpu.make_async_copy(displacements, disp, load.at[4]),
        pltpu.make_async_copy(phases, table, load.at[5]),
        pltpu.make_async_copy(slots_hbm, slots, load.at[6]),
        pltpu.make_async_copy(checkpoint_hbm, checkpoint, load.at[7]),
    ]
    for copy in loads:
        copy.start()
    ring = [target(x, (z + k // 2) & 7, y, (core + k % 2) & 1) for k in range(1, 16)]
    plane = [target((x + k // 4) & 3, z, (y + k % 4) & 3, core) for k in range(1, 16)]
    barrier = pltpu.get_barrier_semaphore()
    for to in ring + plane:
        pl.semaphore_signal(barrier, inc=1, device_id=to, device_id_type=MESH)
    loads[0].wait()
    loads[1].wait()
    pack(cin, c_send0, False)
    pl.semaphore_wait(barrier, 30)
    for to in plane:
        pl.semaphore_signal(ready, inc=1, device_id=to, device_id_type=MESH)
    turn_over(cin, turned)
    pack(turned, c_send1, False)
    pl.semaphore_wait(ready, 15)
    c_sems = (sem.at[pl.ds(0, 2)], sem.at[pl.ds(2, 2)])
    r_sems = (sem.at[pl.ds(4, 2)], sem.at[pl.ds(6, 2)])
    send_near(c_send, c_recv, *c_sems)

    for copy in loads[4:]:
        copy.wait()
    start = checkpoint[0]
    first, second = [], []
    for layer in range(2):
        angle = table[slots[start + layer]]
        cosine, sine = jnp.cos(angle), jnp.sin(angle)
        for mode, held in ((0, first), (1, second)):
            re, im = disp[start + layer, mode, 0], disp[start + layer, mode, 1]
            c, s = cosine[mode : mode + 1], sine[mode : mode + 1]
            held.append((re * c - im * s, re * s + im * c))
    va, wa = first
    vb, wb = second
    ua, ub = cmul(wa, va), cmul(wb, vb)
    gh, gl = split(jnp.concatenate([ua[0].T, ua[1].T], axis=0))
    g3[...] = jnp.concatenate([gh, gh, gl], axis=1)
    spread = (
        lax.broadcasted_iota(jnp.int32, (128, 64), 0) // 2 == lax.broadcasted_iota(jnp.int32, (128, 64), 1)
    ).astype(F32)
    parity = (
        lax.broadcasted_iota(jnp.int32, (128, 128), 0) + lax.broadcasted_iota(jnp.int32, (128, 128), 1)
    ) % 2 == 0

    def both(m):
        wide = dot(dot(spread, m, NN, HIGHEST), spread, NT, HIGHEST)
        return jnp.where(parity, wide, 0.0)

    ub, vb, wb = [(both(m[0]), both(m[1])) for m in (ub, vb, wb)]
    left = jnp.concatenate([jnp.concatenate([ub[0], -ub[1]], axis=1), jnp.concatenate([ub[1], ub[0]], axis=1)], axis=0)
    right = jnp.concatenate([jnp.concatenate([ub[0], ub[1]], axis=1), jnp.concatenate([-ub[1], ub[0]], axis=1)], axis=0)
    for m, high, low in ((left, left_hi, left_lo), (right, right_hi, right_lo)):
        for other in range(2):
            high[other], low[other] = split(m.T if other else m)

    loads[2].wait()
    loads[3].wait()
    rho_stage(rin, work, right_hi, right_lo, left_hi, left_lo)
    pack(work, r_send0, True)
    turn_over(work, turned)
    pack(turned, r_send1, True)
    send_near(r_send, r_recv, *r_sems)

    wait_near(c_recv, c_sems[1])
    flip(c_recv1, t1, c_recv0)
    mode_one(t1, t2, g3, False)
    flip(t2, t1)
    mode_one(t1, t2, g3, True)
    flip(t2, t3)
    blend(t3, t2, send_a, send_b)
    send_all(send_a, recv_a, sem.at[8], sem.at[9])
    send_all(send_b, recv_b, sem.at[10], sem.at[11])

    flip(c_recv0, t2, c_recv1, False)
    mode_one(t2, t3, g3, True)
    flip(t3, t2)
    wait_near(r_recv, r_sems[1])
    flip(r_recv1, t3, r_recv0)
    flip(t3, t4)
    f = gram(t1, t4, 1.0) + gram(t2, t3, -1.0)
    row0, row1 = diagonals(ua, va, wa, (f[:64], f[64:]))

    total = jnp.zeros((256, 256), F32)
    stores = []
    for a0, (recv, number) in enumerate(((recv_a, 9), (recv_b, 11))):
        wait_tiles(recv, sem.at[number], TILES - 1)
        unpack(recv, work, lower)
        total = final_stage(
            work, lower, rin, right_hi, right_lo, left_hi, left_lo, result, pl.ds(a0 * 128, 128), total
        )
        for ri in range(2):
            rows = pl.ds(a0 * 128, 128)
            copy = pltpu.make_async_copy(result.at[ri, rows], out.at[ri, rows], load.at[a0 * 2 + ri])
            copy.start()
            stores.append(copy)
    j = (total[:128, :128] + total[128:, 128:], total[128:, :128] - total[:128, 128:])
    row2, row3 = diagonals(ub, vb, wb, j)
    blank = jnp.zeros((1, 64), F32)
    tile_ref[0] = jnp.concatenate(
        [jnp.concatenate([row0, blank], axis=1), jnp.concatenate([row1, blank], axis=1), row2, row3,
         jnp.zeros((4, 128), F32)], axis=0)

    for half, (group, held) in enumerate(((ring, near), (plane, far))):
        for k, to in enumerate(group):
            pltpu.make_async_remote_copy(
                src_ref=tile_ref.at[half], dst_ref=held.at[k], send_sem=sem.at[12 + half],
                recv_sem=sem.at[14 + half], device_id=to, device_id_type=MESH,
            ).start()
        pltpu.make_async_copy(held, held, sem.at[14 + half]).wait()
        value = tile_ref[half]
        for k in range(15):
            value = value + held[k]
        tile_ref[half + 1] = value
    summed = tile_ref[2]
    modes = dot(summed, spread, NN, HIGHEST)
    for layer in range(2):
        grads[layer, 0:1, :] = summed[layer : layer + 1, :64]
        grads[layer, 1:2, :] = modes[2 + layer : 3 + layer, :]
    for half, held in enumerate((near, far)):
        pltpu.make_async_copy(held, held, sem.at[12 + half]).wait()
    wait_near_sent(c_send, c_sems[0])
    wait_near_sent(r_send, r_sems[0])
    wait_tiles(send_a, sem.at[8], TILES - 1)
    wait_tiles(send_b, sem.at[10], TILES - 1)
    for copy in stores:
        copy.wait()


def per_device(density, costate, phases, displacements, table_slot, checkpoint):
    anywhere = pl.BlockSpec(memory_space=pl.ANY)
    vmem = pl.BlockSpec(memory_space=pltpu.VMEM)
    field = pltpu.VMEM((2, 256, 1024), F32)
    tiles = pltpu.VMEM((8 * TILES, 128), F32)
    spaced = pltpu.VMEM((32 * PITCH, 128), F32)
    matrix = pltpu.VMEM((2, 256, 256), BF16)
    return pl.pallas_call(
        kernel,
        out_shape=(jax.ShapeDtypeStruct(costate.shape, F32), jax.ShapeDtypeStruct((2, 2, LEVELS), F32)),
        in_specs=[anywhere] * 6,
        out_specs=(anywhere, vmem),
        scratch_shapes=[field] * 5
        + [
            pltpu.VMEM((2, 128, 1024), F32),
            pltpu.VMEM(displacements.shape, F32),
            pltpu.VMEM(phases.shape, F32),
            pltpu.SMEM(table_slot.shape, jnp.int32),
            pltpu.SMEM(checkpoint.shape, jnp.int32),
        ]
        + [tiles] * 4 + [spaced] * 4 + [tiles] * 4 + [spaced] * 4
        + [pltpu.VMEM((128, 192), BF16)]
        + [matrix] * 4
        + [
            pltpu.VMEM((3, 8, 128), F32),
            pltpu.VMEM((15, 8, 128), F32),
            pltpu.VMEM((15, 8, 128), F32),
            pltpu.SemaphoreType.REGULAR,
            pltpu.SemaphoreType.DMA((8,)),
            pltpu.SemaphoreType.DMA((16,)),
        ],
        compiler_params=pltpu.CompilerParams(
            collective_id=0, has_side_effects=True, vmem_limit_bytes=52 * 2**20
        ),
    )(density, costate, phases, displacements, table_slot, checkpoint)


def solution(mesh):
    return jax.shard_map(
        per_device,
        mesh=mesh,
        in_specs=(P(None, "dev", "grp"), P(None, "dev", "grp"), P(), P(), P(), P()),
        out_specs=(P(None, "dev", "grp"), P()),
        check_vma=False,
    )
```

```python
import functools

import jax
import jax.numpy as jnp
from jax import lax
from jax.experimental import pallas as pl
from jax.experimental.pallas import tpu as pltpu
from jax.sharding import PartitionSpec as P

LEVELS = 64
TILES = 256
PITCH = 72
MESH = pl.DeviceIdType.MESH
HIGHEST = lax.Precision.HIGHEST
F32 = jnp.float32
BF16 = jnp.bfloat16
NN = ((1,), (0,))
NT = ((1,), (1,))


def dot(a, b, dims=NN, precision=None):
    return lax.dot_general(a, b, (dims, ((), ())), precision=precision, preferred_element_type=F32)


def split(x):
    high = x.astype(BF16)
    return high, (x - high.astype(F32)).astype(BF16)


def dot3(a, b, dims=NN):
    return dot(a[0], b[0], dims) + dot(a[0], b[1], dims) + dot(a[1], b[0], dims)


def roll(x, shift):
    return pltpu.roll(x, shift % 128, 1)


def lane(rows=8):
    return lax.broadcasted_iota(jnp.int32, (rows, 128), 1)


def swap_bit(a, b, weight, low):
    return jnp.where(low, a, roll(b, weight)), jnp.where(low, roll(a, -weight), b)


def place():
    g = lax.axis_index("grp")
    d = lax.axis_index("dev")
    return d >> 3, ((d >> 2) & 1) * 4 + (g >> 1), d & 3, g & 1


def target(x, z, y, core):
    return (z & 3) * 2 + core, x * 8 + (z >> 2) * 4 + y


def apart(a, b):
    e = (a - b) & 7
    return jnp.minimum(e, 8 - e)


def tile(t):
    return pl.ds(pl.multiple_of(t * 8, 8), 8)


def slot(d, g):
    return pl.ds(pl.multiple_of(d * PITCH + g * 8, 8), 8)


def visit(act, k, steps):
    x, z, y, core = place()
    tx, ty, tc = (x + k) & 3, (y + (k >> 2)) & 3, (core + (k >> 4)) & 1
    for dz in steps:
        g, d = target(tx, (z + dz) & 7, ty, tc)
        act(g, d, dz, (tx + ty + tc) & 1)


ALL = (0, 4, 1, 5, 2, 6, 3, 7)
AWAY = (4, 1, 5, 2, 6, 3, 7)


def visit_range(act, low, high, steps=ALL):
    def body(k, carry):
        visit(act, k, steps)
        return carry

    lax.fori_loop(low, high, body, 0)


def for_first(act):
    visit(act, 0, AWAY)
    visit(act, 16, ALL)
    visit_range(act, 1, 16, (0,))


def for_rest(act):
    visit_range(act, 1, 16, AWAY)
    visit_range(act, 17, 32)


def for_others(act):
    visit(act, 0, AWAY)
    visit_range(act, 1, 32)


def send_some(send, recv, send_sem, recv_sem, low, high):
    me_g, me_d = lax.axis_index("grp"), lax.axis_index("dev")

    def act(g, d, dz, parity):
        pltpu.make_async_remote_copy(
            src_ref=send.at[slot(d, g)],
            dst_ref=recv.at[tile(me_d * 8 + me_g)],
            send_sem=send_sem,
            recv_sem=recv_sem,
            device_id=(g, d),
            device_id_type=MESH,
        ).start()

    if low == 0:
        visit(act, 0, AWAY)
        recv[tile(me_d * 8 + me_g), :] = send[slot(me_d, me_g), :]
    visit_range(act, max(low, 1), high)


def send_near(order, send, recv, send_sem, recv_sem, visits):
    x, z, y, core = place()
    me_g, me_d = lax.axis_index("grp"), lax.axis_index("dev")
    quad = me_d >> 2
    alone = quad == me_g
    after = (quad > me_g).astype(jnp.int32)
    other = core * 4 + x
    nearer = []
    for dz in range(8):
        own, far = min(dz, 8 - dz), apart(other, z + dz)
        nearer.append(jnp.where(far == own, 2, jnp.where(own < far, 1, 0)))

    def act(g, d, dz, parity):
        chosen = jnp.where(nearer[dz] == 2, parity ^ after, nearer[dz]) == 1

        @pl.when(alone | chosen if order == 0 else jnp.logical_not(alone) & chosen)
        def _():
            pltpu.make_async_remote_copy(
                src_ref=send[order].at[tile(d * 8 + g)],
                dst_ref=recv[order].at[slot(me_d, me_g)],
                send_sem=send_sem.at[order],
                recv_sem=recv_sem.at[order],
                device_id=(g, d),
                device_id_type=MESH,
            ).start()

    for each in visits:
        each(act)
    recv[order][slot(me_d, me_g), :] = send[order][tile(me_d * 8 + me_g), :]


def wait_tiles(ref, sem, count):
    rest = ref.at[pl.ds(0, 8 * count)]
    pltpu.make_async_copy(rest, rest, sem).wait()


def wait_near(recv, recv_sem):
    alone = lax.axis_index("dev") >> 2 == lax.axis_index("grp")
    wait_tiles(recv[0], recv_sem.at[0], 143)
    for flag, count in ((alone, 112), (jnp.logical_not(alone), 111)):

        @pl.when(flag)
        def _(count=count):
            wait_tiles(recv[1], recv_sem.at[1], count)


def wait_near_sent(send, send_sem):
    alone = lax.axis_index("dev") >> 2 == lax.axis_index("grp")

    @pl.when(alone)
    def _():
        wait_tiles(send[0], send_sem.at[0], 255)

    @pl.when(jnp.logical_not(alone))
    def _():
        wait_tiles(send[0], send_sem.at[0], 127)
        wait_tiles(send[1], send_sem.at[1], 127)


def columns(index, width=128):
    return pl.ds(pl.multiple_of(index * width, width), width)


def masks(bo):
    ln = lane()
    window = (ln >= 8 * bo) & (ln < 8 * bo + 64)
    diagonal = ((ln & 63) >= 8 * bo) & ((ln & 63) < 8 * bo + 8)
    return ln < 64, ln & 32 == 0, window, diagonal


def quarter(rows=8):
    return jnp.where(lane(rows) < 64, -1.0, 1.0).astype(F32)


def pack(field, send, half_diagonal):
    sgn = quarter()

    def body(al, carry):
        for bo in range(8):
            low64, low32, window, diagonal = masks(bo)
            v = [[], []]
            for a0 in range(2):
                folded = []
                for rb in range(2):
                    rows = pl.ds(a0 * 128 + rb * 64 + bo * 8, 8)
                    re, im = [field[ri, rows, columns(al)] for ri in range(2)]
                    a = jnp.where(low64, re, im)
                    b = roll(jnp.where(low64, im, re), 64)
                    keep = window if rb == 0 else jnp.logical_not(window)
                    folded.append(jnp.where(keep, a, b))
                    if rb == 0:
                        rest = jnp.where(window, b, a)
                k = folded[0] + sgn * roll(folded[1], 64)
                if half_diagonal:
                    k = 0.5 * k
                v[0].append(jnp.where(diagonal, k, folded[0]))
                v[1].append(jnp.where(diagonal, rest, folded[1]))
            for rb in range(2):
                w = swap_bit(v[rb][0], v[rb][1], 32, low32)
                for h in range(2):
                    send[pl.ds(h * 1024 + rb * 512 + bo * 64 + al, 8, stride=8), :] = w[h]
        return carry

    lax.fori_loop(0, 8, body, 0)


def turn_over(field, dst):
    def body(al, carry):
        for a0 in range(2):
            rows = pl.ds(a0 * 128, 128)
            dst[0, rows, columns(al)] = field[0, rows, columns(al)].T
            dst[1, rows, columns(al)] = -(field[1, rows, columns(al)].T)
        return carry

    lax.fori_loop(0, 8, body, 0)


def unpack(recv, dst, turned):
    sgn = quarter()
    way = 0.5 if turned else -0.5

    def body(al, carry):
        for bo in range(8):
            low64, low32, window, diagonal = masks(bo)
            outside = diagonal & jnp.logical_not(low64)
            v = []
            for rb in range(2):
                t = [recv[pl.ds(h * 1024 + rb * 512 + bo * 64 + al, 8, stride=8), :] for h in range(2)]
                v.append(swap_bit(t[0], t[1], 32, low32))
            for a0 in range(2):
                v0, v1 = v[0][a0], v[1][a0]
                if turned:
                    v0, v1 = -sgn * v0, -sgn * v1
                r0, r1 = roll(v0, 64), roll(v1, 64)
                u0, s0 = jnp.where(diagonal, 0.5 * v0, v0), jnp.where(diagonal, 0.5 * r0, r0)
                u1, s1 = jnp.where(diagonal, way * sgn * r0, v1), jnp.where(diagonal, -way * sgn * v0, r1)
                rows = pl.ds(a0 * 128 + bo * 8, 8)
                dst[0, rows, columns(al)] = jnp.where(window, jnp.where(low64, u0, s0), jnp.where(outside, r1, 0.0))
                dst[1, rows, columns(al)] = jnp.where(window, jnp.where(low64, s0, u0), jnp.where(outside, v1, 0.0))
                rows = pl.ds(a0 * 128 + 64 + bo * 8, 8)
                dst[0, rows, columns(al)] = jnp.where(window, 0.0, jnp.where(low64, u1, s1))
                dst[1, rows, columns(al)] = jnp.where(window, 0.0, jnp.where(low64, s1, u1))
        return carry

    lax.fori_loop(0, 8, body, 0)


def mode_one(src, dst, g3, conjugate):
    sgn = quarter(64)
    if conjugate:
        sgn = -sgn

    def body(i, carry):
        base = pl.multiple_of(i * (8 * PITCH), 8)
        for j in range(2):
            rows = [pl.ds(base + (4 * j + k) * PITCH, 64) for k in range(4)]
            x = jnp.concatenate([src[r, :] for r in rows], axis=1)
            high, low = split(x)
            p = dot(g3[...], jnp.concatenate([high, low, high], axis=0))
            for k in range(4):
                q = p[:, k * 128 : k * 128 + 128]
                dst[rows[k], :] = q[:64] + sgn * roll(q[64:], 64)
        return carry

    lax.fori_loop(0, 4, body, 0)


def sent_direct(quad, k, alone):
    x, z, y, core = place()
    g = 2 * k + (lax.broadcasted_iota(jnp.int32, (8, 128), 0) >> 2)
    own = apart((quad & 1) * 4 + (g >> 1), z)
    far = apart((g & 1) * 4 + (quad >> 1), z)
    parity = (x + y + core) & 1
    tie = jnp.where(quad > g, 1, 0) != parity
    chosen = (own < far) | ((own == far) & tie)
    return (quad == g) | chosen if alone else (quad != g) & chosen


def flip(src, dst, direct=None, alone=True):
    low32 = lane() & 32 == 0

    def body(quad, carry):
        for k in range(4):
            if direct is not None:
                keep = sent_direct(quad, k, alone)
            for j in range(4):
                c = quad * 4 + j
                e = [src[pl.ds(k * (8 * PITCH) + c * 2 + bit, 8, stride=PITCH), :] for bit in range(2)]
                o = swap_bit(e[0], e[1], 32, low32)
                for bit in range(2):
                    rows = pl.ds(c * PITCH + k * 16 + bit, 8, stride=2)
                    value = o[bit]
                    if direct is not None:
                        value = jnp.where(keep, direct[rows, :], value)
                    dst[rows, :] = value
        return carry

    lax.fori_loop(0, 8, body, 0)


def gram(x_ref, y_ref, flag):
    sgn = quarter(64) * (-flag)

    def body(i, acc):
        xs, ys = [], []
        for k in range(4):
            rows = pl.ds(pl.multiple_of(i * (4 * PITCH), 8) + k * PITCH, 64)
            x = x_ref[rows, :]
            xh, xl = split(jnp.concatenate([x, sgn * roll(x, 64)], axis=0))
            yh, yl = split(y_ref[rows, :])
            xs += [xh, xh, xl, xl]
            ys += [yh, yl, yh, yl]
        return acc + dot(jnp.concatenate(xs, axis=1), jnp.concatenate(ys, axis=1), NT)

    return lax.fori_loop(0, 8, body, jnp.zeros((128, 64), F32))


def cmul(a, b, dims=NN):
    mul = functools.partial(dot, dims=dims, precision=HIGHEST)
    return mul(a[0], b[0]) - mul(a[1], b[1]), mul(a[0], b[1]) + mul(a[1], b[0])


def conj(a):
    return a[0], -a[1]


def diagonals(u, v, w, m):
    t = cmul(m, conj(v), NT)
    first = jnp.sum(u[0] * m[1] - u[1] * m[0], axis=0, keepdims=True)
    second = jnp.sum(w[0] * t[1] - w[1] * t[0], axis=0, keepdims=True)
    return 2.0 * first, 2.0 * second


def across(x, right_hi, right_lo):
    t = []
    for k in range(2):
        piece = jnp.concatenate([q[:, k * 128 : k * 128 + 128] for q in x], axis=1)
        t.append(dot3(split(piece), (right_hi, right_lo)))
    return [jnp.concatenate([q[:, half * 128 : half * 128 + 128] for q in t], axis=1) for half in range(2)]


def rho_stage(rin, work, right_hi, right_lo, left_hi, left_lo):
    def body(i, carry):
        wide = columns(i, 256)
        t = across([rin[ri, :, wide] for ri in range(2)], right_hi[1], right_lo[1])
        for a0 in range(2):
            rows = pl.ds(a0 * 128, 128)
            y = dot3((left_hi[0], left_lo[0]), split(jnp.concatenate(halves(t, a0), axis=0)))
            work[0, rows, wide] = y[:128]
            work[1, rows, wide] = y[128:]
        return carry

    lax.fori_loop(0, 4, body, 0)


def halves(x, a0):
    return [q[a0 * 128 : a0 * 128 + 128] for q in x]


def lower_stage(lower, rin, right_hi, right_lo, left_hi, left_lo, result):
    def body(i, acc):
        first, second = acc
        wide = columns(i, 256)
        e = [lower[ri, :, wide] for ri in range(2)]
        x = [
            jnp.concatenate(
                [
                    jnp.concatenate([q[a0 * 128 : a0 * 128 + 128, k * 128 : k * 128 + 128].T for k in range(2)], axis=1)
                    for a0 in range(2)
                ],
                axis=0,
            )
            for q in e
        ]
        t = across(x, right_hi[0], right_lo[0])
        w = across([e[0], -e[1]], right_hi[0], right_lo[0])
        for a0 in range(2):
            rows = pl.ds(a0 * 128, 128)
            th, tl = split(jnp.concatenate(halves(t, a0), axis=0))
            y = dot3((left_hi[1], left_lo[1]), (th, tl))
            result[0, rows, wide] = y[:128]
            result[1, rows, wide] = y[128:]
            r = [rin[ri, rows, wide] for ri in range(2)]
            rh, rl = split(jnp.concatenate(r, axis=0))
            first = first + dot3((th, tl), (rh, rl), NT) + dot(tl, rl, NT)
            wh, wl = split(jnp.concatenate(halves(w, a0), axis=0))
            r = [jnp.concatenate([q[:, k * 128 : k * 128 + 128] for q in r], axis=1) for k in range(2)]
            rh, rl = split(jnp.concatenate(r, axis=0))
            second = second + dot3((wh, wl), (rh, rl)) + dot(wl, rl)
        return first, second

    zero = jnp.zeros((256, 256), F32)
    return lax.fori_loop(0, 4, body, (zero, zero))


def upper_stage(upper, right_hi, right_lo, left_hi, left_lo, result, out, stored):
    def body(i, carry):
        wide = columns(i, 256)
        t = across([upper[ri, :, wide] for ri in range(2)], right_hi[0], right_lo[0])
        for a0 in range(2):
            rows = pl.ds(a0 * 128, 128)
            y = dot3((left_hi[1], left_lo[1]), split(jnp.concatenate(halves(t, a0), axis=0)))
            result[0, rows, wide] += y[:128]
            result[1, rows, wide] += y[128:]
        pltpu.make_async_copy(result.at[:, :, wide], out.at[:, :, wide], stored.at[i]).start()
        return carry

    lax.fori_loop(0, 4, body, 0)


def kernel(
    density, costate, phases, displacements, slots_hbm, checkpoint_hbm, out, grads,
    result, cin, rin, work, turned, disp, table, slots, checkpoint,
    c_send0, c_send1, r_send0, r_send1, recv_l, recv_u,
    c_recv0, c_recv1, r_recv0, r_recv1, t1, t2, t3, t4, t5, t6, g3, left_hi, left_lo, right_hi, right_lo, tile_ref, near, far,
    ready, load, sem,
):
    c_send, r_send = (c_send0, c_send1), (r_send0, r_send1)
    c_recv, r_recv = (c_recv0, c_recv1), (r_recv0, r_recv1)
    x, z, y, core = place()
    loads = [
        pltpu.make_async_copy(costate.at[0], cin.at[0], load.at[0]),
        pltpu.make_async_copy(costate.at[1], cin.at[1], load.at[1]),
        pltpu.make_async_copy(density.at[0], rin.at[0], load.at[2]),
        pltpu.make_async_copy(density.at[1], rin.at[1], load.at[3]),
        pltpu.make_async_copy(displacements, disp, load.at[4]),
        pltpu.make_async_copy(phases, table, load.at[5]),
        pltpu.make_async_copy(slots_hbm, slots, load.at[6]),
        pltpu.make_async_copy(checkpoint_hbm, checkpoint, load.at[7]),
    ]
    for copy in loads:
        copy.start()
    ring = [target(x, (z + k // 2) & 7, y, (core + k % 2) & 1) for k in range(1, 16)]
    plane = [target((x + k // 4) & 3, z, (y + k % 4) & 3, core) for k in range(1, 16)]
    barrier = pltpu.get_barrier_semaphore()
    for to in ring + plane:
        pl.semaphore_signal(barrier, inc=1, device_id=to, device_id_type=MESH)
    loads[0].wait()
    loads[1].wait()
    pack(cin, c_send0, False)
    pl.semaphore_wait(barrier, 30)
    for to in plane:
        pl.semaphore_signal(ready, inc=1, device_id=to, device_id_type=MESH)
    c_sems = (sem.at[pl.ds(0, 2)], sem.at[pl.ds(2, 2)])
    r_sems = (sem.at[pl.ds(4, 2)], sem.at[pl.ds(6, 2)])
    send_near(0, c_send, c_recv, *c_sems, (for_first, lambda act: pl.semaphore_wait(ready, 15), for_rest))
    turn_over(cin, turned)
    pack(turned, c_send1, False)
    send_near(1, c_send, c_recv, *c_sems, (for_others,))

    for copy in loads[4:]:
        copy.wait()
    start = checkpoint[0]
    first, second = [], []
    for layer in range(2):
        angle = table[slots[start + layer]]
        cosine, sine = jnp.cos(angle), jnp.sin(angle)
        for mode, held in ((0, first), (1, second)):
            re, im = disp[start + layer, mode, 0], disp[start + layer, mode, 1]
            c, s = cosine[mode : mode + 1], sine[mode : mode + 1]
            held.append((re * c - im * s, re * s + im * c))
    va, wa = first
    vb, wb = second
    ua, ub = cmul(wa, va), cmul(wb, vb)
    gh, gl = split(jnp.concatenate([ua[0].T, ua[1].T], axis=0))
    g3[...] = jnp.concatenate([gh, gh, gl], axis=1)
    spread = (
        lax.broadcasted_iota(jnp.int32, (128, 64), 0) // 2 == lax.broadcasted_iota(jnp.int32, (128, 64), 1)
    ).astype(F32)
    parity = (
        lax.broadcasted_iota(jnp.int32, (128, 128), 0) + lax.broadcasted_iota(jnp.int32, (128, 128), 1)
    ) % 2 == 0

    def both(m):
        wide = dot(dot(spread, m, NN, HIGHEST), spread, NT, HIGHEST)
        return jnp.where(parity, wide, 0.0)

    ub, vb, wb = [(both(m[0]), both(m[1])) for m in (ub, vb, wb)]
    left = jnp.concatenate([jnp.concatenate([ub[0], -ub[1]], axis=1), jnp.concatenate([ub[1], ub[0]], axis=1)], axis=0)
    right = jnp.concatenate([jnp.concatenate([ub[0], ub[1]], axis=1), jnp.concatenate([-ub[1], ub[0]], axis=1)], axis=0)
    for m, high, low in ((left, left_hi, left_lo), (right, right_hi, right_lo)):
        for other in range(2):
            high[other], low[other] = split(m.T if other else m)

    loads[2].wait()
    loads[3].wait()
    rho_stage(rin, work, right_hi, right_lo, left_hi, left_lo)
    pack(work, r_send0, True)
    send_near(0, r_send, r_recv, *r_sems, (for_others,))
    turn_over(work, turned)
    pack(turned, r_send1, True)
    send_near(1, r_send, r_recv, *r_sems, (for_others,))

    wait_near(c_recv, c_sems[1])
    flip(c_recv1, t1, c_recv0)
    mode_one(t1, t2, g3, False)
    flip(t2, t1)
    mode_one(t1, t2, g3, True)
    send_some(t2, recv_l, sem.at[8], sem.at[9], 0, 32)
    flip(t2, t3)

    flip(c_recv0, t4, c_recv1, False)
    mode_one(t4, t5, g3, True)
    flip(t5, t4)
    wait_near(r_recv, r_sems[1])
    flip(r_recv1, t5, r_recv0)
    flip(t5, t6)
    f = gram(t1, t6, 1.0) + gram(t4, t5, -1.0)
    row0, row1 = diagonals(ua, va, wa, (f[:64], f[64:]))

    send_some(t3, recv_u, sem.at[10], sem.at[11], 0, 19)
    wait_tiles(recv_l, sem.at[9], TILES - 1)
    unpack(recv_l, work, True)
    m, n = lower_stage(work, rin, right_hi, right_lo, left_hi, left_lo, result)
    j = (
        m[:128, :128] + m[128:, 128:] + n[:128, :128] - n[128:, 128:],
        m[128:, :128] - m[:128, 128:] + n[:128, 128:] + n[128:, :128],
    )
    row2, row3 = diagonals(ub, vb, wb, j)
    blank = jnp.zeros((1, 64), F32)
    tile_ref[0] = jnp.concatenate(
        [jnp.concatenate([row0, blank], axis=1), jnp.concatenate([row1, blank], axis=1), row2, row3,
         jnp.zeros((4, 128), F32)], axis=0)

    def spread_out(half, group, held):
        for k, to in enumerate(group):
            pltpu.make_async_remote_copy(
                src_ref=tile_ref.at[half], dst_ref=held.at[k], send_sem=sem.at[12 + half],
                recv_sem=sem.at[14 + half], device_id=to, device_id_type=MESH,
            ).start()

    def add_up(half, held):
        pltpu.make_async_copy(held, held, sem.at[14 + half]).wait()
        value = tile_ref[half]
        for k in range(15):
            value = value + held[k]
        tile_ref[half + 1] = value

    spread_out(0, ring, near)
    send_some(t3, recv_u, sem.at[10], sem.at[11], 19, 32)
    add_up(0, near)
    spread_out(1, plane, far)

    wait_tiles(recv_u, sem.at[11], TILES - 1)
    unpack(recv_u, work, False)
    upper_stage(work, right_hi, right_lo, left_hi, left_lo, result, out, load)

    add_up(1, far)
    summed = tile_ref[2]
    modes = dot(summed, spread, NN, HIGHEST)
    for layer in range(2):
        grads[layer, 0:1, :] = summed[layer : layer + 1, :64]
        grads[layer, 1:2, :] = modes[2 + layer : 3 + layer, :]
    for half, held in enumerate((near, far)):
        pltpu.make_async_copy(held, held, sem.at[12 + half]).wait()
    wait_near_sent(c_send, c_sems[0])
    wait_near_sent(r_send, r_sems[0])
    wait_tiles(t2, sem.at[8], TILES - 1)
    wait_tiles(t3, sem.at[10], TILES - 1)
    for k in range(4):
        wide = pl.ds(k * 256, 256)
        pltpu.make_async_copy(result.at[:, :, wide], out.at[:, :, wide], load.at[k]).wait()


def per_device(density, costate, phases, displacements, table_slot, checkpoint):
    anywhere = pl.BlockSpec(memory_space=pl.ANY)
    vmem = pl.BlockSpec(memory_space=pltpu.VMEM)
    field = pltpu.VMEM((2, 256, 1024), F32)
    tiles = pltpu.VMEM((8 * TILES, 128), F32)
    spaced = pltpu.VMEM((32 * PITCH, 128), F32)
    matrix = pltpu.VMEM((2, 256, 256), BF16)
    return pl.pallas_call(
        kernel,
        out_shape=(jax.ShapeDtypeStruct(costate.shape, F32), jax.ShapeDtypeStruct((2, 2, LEVELS), F32)),
        in_specs=[anywhere] * 6,
        out_specs=(anywhere, vmem),
        scratch_shapes=[field] * 5
        + [
            pltpu.VMEM(displacements.shape, F32),
            pltpu.VMEM(phases.shape, F32),
            pltpu.SMEM(table_slot.shape, jnp.int32),
            pltpu.SMEM(checkpoint.shape, jnp.int32),
        ]
        + [tiles] * 6 + [spaced] * 10
        + [pltpu.VMEM((128, 192), BF16)]
        + [matrix] * 4
        + [
            pltpu.VMEM((3, 8, 128), F32),
            pltpu.VMEM((15, 8, 128), F32),
            pltpu.VMEM((15, 8, 128), F32),
            pltpu.SemaphoreType.REGULAR,
            pltpu.SemaphoreType.DMA((8,)),
            pltpu.SemaphoreType.DMA((16,)),
        ],
        compiler_params=pltpu.CompilerParams(
            collective_id=0, has_side_effects=True, vmem_limit_bytes=50 * 2**20
        ),
    )(density, costate, phases, displacements, table_slot, checkpoint)


def solution(mesh):
    return jax.shard_map(
        per_device,
        mesh=mesh,
        in_specs=(P(None, "dev", "grp"), P(None, "dev", "grp"), P(), P(), P(), P()),
        out_specs=(P(None, "dev", "grp"), P()),
        check_vma=False,
    )
```

```python
import functools

import jax
import jax.numpy as jnp
from jax import lax
from jax.experimental import pallas as pl
from jax.experimental.pallas import tpu as pltpu
from jax.sharding import PartitionSpec as P

LEVELS = 64
TILES = 256
PITCH = 72
MESH = pl.DeviceIdType.MESH
HIGHEST = lax.Precision.HIGHEST
F32 = jnp.float32
BF16 = jnp.bfloat16
NN = ((1,), (0,))
NT = ((1,), (1,))


def dot(a, b, dims=NN, precision=None):
    return lax.dot_general(a, b, (dims, ((), ())), precision=precision, preferred_element_type=F32)


def split(x):
    high = x.astype(BF16)
    return high, (x - high.astype(F32)).astype(BF16)


def dot3(a, b, dims=NN):
    return dot(a[0], b[0], dims) + dot(a[0], b[1], dims) + dot(a[1], b[0], dims)


def roll(x, shift):
    return pltpu.roll(x, shift % 128, 1)


def lane(rows=8):
    return lax.broadcasted_iota(jnp.int32, (rows, 128), 1)


def swap_bit(a, b, weight, low):
    return jnp.where(low, a, roll(b, weight)), jnp.where(low, roll(a, -weight), b)


def place():
    g = lax.axis_index("grp")
    d = lax.axis_index("dev")
    return d >> 3, ((d >> 2) & 1) * 4 + (g >> 1), d & 3, g & 1


def target(x, z, y, core):
    return (z & 3) * 2 + core, x * 8 + (z >> 2) * 4 + y


def apart(a, b):
    e = (a - b) & 7
    return jnp.minimum(e, 8 - e)


def tile(t):
    return pl.ds(pl.multiple_of(t * 8, 8), 8)


def slot(d, g):
    return pl.ds(pl.multiple_of(d * PITCH + g * 8, 8), 8)


def visit(act, k, steps):
    x, z, y, core = place()
    tx, ty, tc = (x + k) & 3, (y + (k >> 2)) & 3, (core + (k >> 4)) & 1
    for dz in steps:
        g, d = target(tx, (z + dz) & 7, ty, tc)
        act(g, d, dz, (tx + ty + tc) & 1)


ALL = (0, 4, 1, 5, 2, 6, 3, 7)
AWAY = (4, 1, 5, 2, 6, 3, 7)


def visit_range(act, low, high, steps=ALL):
    def body(k, carry):
        visit(act, k, steps)
        return carry

    lax.fori_loop(low, high, body, 0)


def for_first(act):
    visit(act, 0, AWAY)
    visit(act, 16, ALL)
    visit_range(act, 1, 16, (0,))


def for_rest(act):
    visit_range(act, 1, 16, AWAY)
    visit_range(act, 17, 32)


def for_others(act):
    visit(act, 0, AWAY)
    visit_range(act, 1, 32)


def send_some(send, recv, send_sem, recv_sem, low, high):
    me_g, me_d = lax.axis_index("grp"), lax.axis_index("dev")

    def act(g, d, dz, parity):
        pltpu.make_async_remote_copy(
            src_ref=send.at[slot(d, g)],
            dst_ref=recv.at[tile(me_d * 8 + me_g)],
            send_sem=send_sem,
            recv_sem=recv_sem,
            device_id=(g, d),
            device_id_type=MESH,
        ).start()

    if low == 0:
        visit(act, 0, AWAY)
        recv[tile(me_d * 8 + me_g), :] = send[slot(me_d, me_g), :]
    visit_range(act, max(low, 1), high)


def send_near(order, send, recv, send_sem, recv_sem, visits):
    x, z, y, core = place()
    me_g, me_d = lax.axis_index("grp"), lax.axis_index("dev")
    quad = me_d >> 2
    alone = quad == me_g
    after = (quad > me_g).astype(jnp.int32)
    other = core * 4 + x
    nearer = []
    for dz in range(8):
        own, far = min(dz, 8 - dz), apart(other, z + dz)
        nearer.append(jnp.where(far == own, 2, jnp.where(own < far, 1, 0)))

    def act(g, d, dz, parity):
        chosen = jnp.where(nearer[dz] == 2, parity ^ after, nearer[dz]) == 1

        @pl.when(alone | chosen if order == 0 else jnp.logical_not(alone) & chosen)
        def _():
            pltpu.make_async_remote_copy(
                src_ref=send[order].at[tile(d * 8 + g)],
                dst_ref=recv[order].at[slot(me_d, me_g)],
                send_sem=send_sem.at[order],
                recv_sem=recv_sem.at[order],
                device_id=(g, d),
                device_id_type=MESH,
            ).start()

    for each in visits:
        each(act)
    recv[order][slot(me_d, me_g), :] = send[order][tile(me_d * 8 + me_g), :]


def wait_tiles(ref, sem, count):
    rest = ref.at[pl.ds(0, 8 * count)]
    pltpu.make_async_copy(rest, rest, sem).wait()


def wait_near(recv, recv_sem):
    alone = lax.axis_index("dev") >> 2 == lax.axis_index("grp")
    wait_tiles(recv[0], recv_sem.at[0], 143)
    for flag, count in ((alone, 112), (jnp.logical_not(alone), 111)):

        @pl.when(flag)
        def _(count=count):
            wait_tiles(recv[1], recv_sem.at[1], count)


def wait_near_sent(send, send_sem):
    alone = lax.axis_index("dev") >> 2 == lax.axis_index("grp")

    @pl.when(alone)
    def _():
        wait_tiles(send[0], send_sem.at[0], 255)

    @pl.when(jnp.logical_not(alone))
    def _():
        wait_tiles(send[0], send_sem.at[0], 127)
        wait_tiles(send[1], send_sem.at[1], 127)


def columns(index, width=128):
    return pl.ds(pl.multiple_of(index * width, width), width)


def masks(bo):
    ln = lane()
    window = (ln >= 8 * bo) & (ln < 8 * bo + 64)
    diagonal = ((ln & 63) >= 8 * bo) & ((ln & 63) < 8 * bo + 8)
    return ln < 64, ln & 32 == 0, window, diagonal


def quarter(rows=8):
    return jnp.where(lane(rows) < 64, -1.0, 1.0).astype(F32)


def pack(field, send, half_diagonal):
    sgn = quarter()

    def body(al, carry):
        for bo in range(8):
            low64, low32, window, diagonal = masks(bo)
            v = [[], []]
            for a0 in range(2):
                folded = []
                for rb in range(2):
                    rows = pl.ds(a0 * 128 + rb * 64 + bo * 8, 8)
                    re, im = [field[ri, rows, columns(al)] for ri in range(2)]
                    a = jnp.where(low64, re, im)
                    b = roll(jnp.where(low64, im, re), 64)
                    keep = window if rb == 0 else jnp.logical_not(window)
                    folded.append(jnp.where(keep, a, b))
                    if rb == 0:
                        rest = jnp.where(window, b, a)
                k = folded[0] + sgn * roll(folded[1], 64)
                if half_diagonal:
                    k = 0.5 * k
                v[0].append(jnp.where(diagonal, k, folded[0]))
                v[1].append(jnp.where(diagonal, rest, folded[1]))
            for rb in range(2):
                w = swap_bit(v[rb][0], v[rb][1], 32, low32)
                for h in range(2):
                    send[pl.ds(h * 1024 + rb * 512 + bo * 64 + al, 8, stride=8), :] = w[h]
        return carry

    lax.fori_loop(0, 8, body, 0)


def turn_over(field, dst):
    def body(al, carry):
        for a0 in range(2):
            rows = pl.ds(a0 * 128, 128)
            dst[0, rows, columns(al)] = field[0, rows, columns(al)].T
            dst[1, rows, columns(al)] = -(field[1, rows, columns(al)].T)
        return carry

    lax.fori_loop(0, 8, body, 0)


def unpack(recv, dst, turned):
    sgn = quarter()
    way = 0.5 if turned else -0.5

    def body(al, carry):
        for bo in range(8):
            low64, low32, window, diagonal = masks(bo)
            outside = diagonal & jnp.logical_not(low64)
            v = []
            for rb in range(2):
                t = [recv[pl.ds(h * 1024 + rb * 512 + bo * 64 + al, 8, stride=8), :] for h in range(2)]
                v.append(swap_bit(t[0], t[1], 32, low32))
            for a0 in range(2):
                v0, v1 = v[0][a0], v[1][a0]
                if turned:
                    v0, v1 = -sgn * v0, -sgn * v1
                r0, r1 = roll(v0, 64), roll(v1, 64)
                u0, s0 = jnp.where(diagonal, 0.5 * v0, v0), jnp.where(diagonal, 0.5 * r0, r0)
                u1, s1 = jnp.where(diagonal, way * sgn * r0, v1), jnp.where(diagonal, -way * sgn * v0, r1)
                rows = pl.ds(a0 * 128 + bo * 8, 8)
                dst[0, rows, columns(al)] = jnp.where(window, jnp.where(low64, u0, s0), jnp.where(outside, r1, 0.0))
                dst[1, rows, columns(al)] = jnp.where(window, jnp.where(low64, s0, u0), jnp.where(outside, v1, 0.0))
                rows = pl.ds(a0 * 128 + 64 + bo * 8, 8)
                dst[0, rows, columns(al)] = jnp.where(window, 0.0, jnp.where(low64, u1, s1))
                dst[1, rows, columns(al)] = jnp.where(window, 0.0, jnp.where(low64, s1, u1))
        return carry

    lax.fori_loop(0, 8, body, 0)


def mode_one(src, dst, g3, conjugate):
    sgn = quarter(64)
    if conjugate:
        sgn = -sgn

    def body(i, carry):
        base = pl.multiple_of(i * (8 * PITCH), 8)
        for j in range(2):
            rows = [pl.ds(base + (4 * j + k) * PITCH, 64) for k in range(4)]
            x = jnp.concatenate([src[r, :] for r in rows], axis=1)
            high, low = split(x)
            p = dot(g3[...], jnp.concatenate([high, low, high], axis=0))
            for k in range(4):
                q = p[:, k * 128 : k * 128 + 128]
                dst[rows[k], :] = q[:64] + sgn * roll(q[64:], 64)
        return carry

    lax.fori_loop(0, 4, body, 0)


def sent_direct(quad, k, alone):
    x, z, y, core = place()
    g = 2 * k + (lax.broadcasted_iota(jnp.int32, (8, 128), 0) >> 2)
    own = apart((quad & 1) * 4 + (g >> 1), z)
    far = apart((g & 1) * 4 + (quad >> 1), z)
    parity = (x + y + core) & 1
    tie = jnp.where(quad > g, 1, 0) != parity
    chosen = (own < far) | ((own == far) & tie)
    return (quad == g) | chosen if alone else (quad != g) & chosen


def flip(src, dst, direct=None, alone=True):
    low32 = lane() & 32 == 0

    def body(quad, carry):
        for k in range(4):
            if direct is not None:
                keep = sent_direct(quad, k, alone)
            for j in range(4):
                c = quad * 4 + j
                e = [src[pl.ds(k * (8 * PITCH) + c * 2 + bit, 8, stride=PITCH), :] for bit in range(2)]
                o = swap_bit(e[0], e[1], 32, low32)
                for bit in range(2):
                    rows = pl.ds(c * PITCH + k * 16 + bit, 8, stride=2)
                    value = o[bit]
                    if direct is not None:
                        value = jnp.where(keep, direct[rows, :], value)
                    dst[rows, :] = value
        return carry

    lax.fori_loop(0, 8, body, 0)


def gram(x_ref, y_ref, flag):
    sgn = quarter(64) * (-flag)

    def body(i, acc):
        xs, ys = [], []
        for k in range(4):
            rows = pl.ds(pl.multiple_of(i * (4 * PITCH), 8) + k * PITCH, 64)
            x = x_ref[rows, :]
            xh, xl = split(jnp.concatenate([x, sgn * roll(x, 64)], axis=0))
            yh, yl = split(y_ref[rows, :])
            xs += [xh, xh, xl, xl]
            ys += [yh, yl, yh, yl]
        return acc + dot(jnp.concatenate(xs, axis=1), jnp.concatenate(ys, axis=1), NT)

    return lax.fori_loop(0, 8, body, jnp.zeros((128, 64), F32))


def cmul(a, b, dims=NN, exact=True):
    mul = functools.partial(dot, dims=dims, precision=HIGHEST)
    if not exact:
        a, b = [[split(q) for q in pair] for pair in (a, b)]
        mul = functools.partial(dot3, dims=dims)
    return mul(a[0], b[0]) - mul(a[1], b[1]), mul(a[0], b[1]) + mul(a[1], b[0])


def conj(a):
    return a[0], -a[1]


def diagonals(u, v, w, m, exact=True):
    t = cmul(m, conj(v), NT, exact)
    first = jnp.sum(u[0] * m[1] - u[1] * m[0], axis=0, keepdims=True)
    second = jnp.sum(w[0] * t[1] - w[1] * t[0], axis=0, keepdims=True)
    return 2.0 * first, 2.0 * second


def across(x, right_hi, right_lo):
    t = []
    for k in range(2):
        piece = jnp.concatenate([q[:, k * 128 : k * 128 + 128] for q in x], axis=1)
        t.append(dot3(split(piece), (right_hi, right_lo)))
    return [jnp.concatenate([q[:, half * 128 : half * 128 + 128] for q in t], axis=1) for half in range(2)]


def rho_stage(rin, work, right_hi, right_lo, left_hi, left_lo):
    def body(i, carry):
        wide = columns(i, 256)
        t = across([rin[ri, :, wide] for ri in range(2)], right_hi[1], right_lo[1])
        for a0 in range(2):
            rows = pl.ds(a0 * 128, 128)
            y = dot3((left_hi[0], left_lo[0]), split(jnp.concatenate(halves(t, a0), axis=0)))
            work[0, rows, wide] = y[:128]
            work[1, rows, wide] = y[128:]
        return carry

    lax.fori_loop(0, 4, body, 0)


def halves(x, a0):
    return [q[a0 * 128 : a0 * 128 + 128] for q in x]


def lower_stage(lower, rin, right_hi, right_lo, across_lower):
    def body(i, acc):
        first, second = acc
        wide = columns(i, 256)
        e = [lower[ri, :, wide] for ri in range(2)]
        x = [
            jnp.concatenate(
                [
                    jnp.concatenate([q[a0 * 128 : a0 * 128 + 128, k * 128 : k * 128 + 128].T for k in range(2)], axis=1)
                    for a0 in range(2)
                ],
                axis=0,
            )
            for q in e
        ]
        t = across(x, right_hi[0], right_lo[0])
        w = across([e[0], -e[1]], right_hi[0], right_lo[0])
        for ri in range(2):
            across_lower[ri, :, wide] = t[ri]
        for a0 in range(2):
            rows = pl.ds(a0 * 128, 128)
            th, tl = split(jnp.concatenate(halves(t, a0), axis=0))
            r = [rin[ri, rows, wide] for ri in range(2)]
            rh, rl = split(jnp.concatenate(r, axis=0))
            first = first + dot3((th, tl), (rh, rl), NT)
            wh, wl = split(jnp.concatenate(halves(w, a0), axis=0))
            r = [jnp.concatenate([q[:, k * 128 : k * 128 + 128] for q in r], axis=1) for k in range(2)]
            rh, rl = split(jnp.concatenate(r, axis=0))
            second = second + dot3((wh, wl), (rh, rl))
        return first, second

    zero = jnp.zeros((256, 256), F32)
    return lax.fori_loop(0, 4, body, (zero, zero))


def down_stage(across_lower, left_hi, left_lo, result):
    def body(i, carry):
        wide = columns(i, 256)
        for a0 in range(2):
            rows = pl.ds(a0 * 128, 128)
            t = [across_lower[ri, rows, wide] for ri in range(2)]
            y = dot3((left_hi[1], left_lo[1]), split(jnp.concatenate(t, axis=0)))
            result[0, rows, wide] = y[:128]
            result[1, rows, wide] = y[128:]
        return carry

    lax.fori_loop(0, 4, body, 0)


def upper_stage(upper, right_hi, right_lo, left_hi, left_lo, result, out, stored):
    def body(i, carry):
        wide = columns(i, 256)
        t = across([upper[ri, :, wide] for ri in range(2)], right_hi[0], right_lo[0])
        for a0 in range(2):
            rows = pl.ds(a0 * 128, 128)
            y = dot3((left_hi[1], left_lo[1]), split(jnp.concatenate(halves(t, a0), axis=0)))
            result[0, rows, wide] += y[:128]
            result[1, rows, wide] += y[128:]
        pltpu.make_async_copy(result.at[:, :, wide], out.at[:, :, wide], stored.at[i]).start()
        return carry

    lax.fori_loop(0, 4, body, 0)


def kernel(
    density, costate, phases, displacements, slots_hbm, checkpoint_hbm, out, grads,
    result, cin, rin, work, turned, disp, table, slots, checkpoint,
    c_send0, c_send1, r_send0, r_send1, recv_l, recv_u,
    c_recv0, c_recv1, r_recv0, r_recv1, t1, t2, t3, t4, t5, t6, g3, left_hi, left_lo, right_hi, right_lo, tile_ref, near, far,
    ready, load, sem,
):
    c_send, r_send = (c_send0, c_send1), (r_send0, r_send1)
    c_recv, r_recv = (c_recv0, c_recv1), (r_recv0, r_recv1)
    x, z, y, core = place()
    loads = [
        pltpu.make_async_copy(costate.at[0], cin.at[0], load.at[0]),
        pltpu.make_async_copy(costate.at[1], cin.at[1], load.at[1]),
        pltpu.make_async_copy(density.at[0], rin.at[0], load.at[2]),
        pltpu.make_async_copy(density.at[1], rin.at[1], load.at[3]),
        pltpu.make_async_copy(displacements, disp, load.at[4]),
        pltpu.make_async_copy(phases, table, load.at[5]),
        pltpu.make_async_copy(slots_hbm, slots, load.at[6]),
        pltpu.make_async_copy(checkpoint_hbm, checkpoint, load.at[7]),
    ]
    for copy in loads:
        copy.start()
    ring = [target(x, (z + k // 2) & 7, y, (core + k % 2) & 1) for k in range(1, 16)]
    plane = [target((x + k // 4) & 3, z, (y + k % 4) & 3, core) for k in range(1, 16)]
    barrier = pltpu.get_barrier_semaphore()
    for to in ring + plane:
        pl.semaphore_signal(barrier, inc=1, device_id=to, device_id_type=MESH)
    loads[0].wait()
    loads[1].wait()
    pack(cin, c_send0, False)
    pl.semaphore_wait(barrier, 30)
    for to in plane:
        pl.semaphore_signal(ready, inc=1, device_id=to, device_id_type=MESH)
    c_sems = (sem.at[pl.ds(0, 2)], sem.at[pl.ds(2, 2)])
    r_sems = (sem.at[pl.ds(4, 2)], sem.at[pl.ds(6, 2)])
    send_near(0, c_send, c_recv, *c_sems, (for_first, lambda act: pl.semaphore_wait(ready, 15), for_rest))
    turn_over(cin, turned)
    pack(turned, c_send1, False)
    send_near(1, c_send, c_recv, *c_sems, (for_others,))

    for copy in loads[4:]:
        copy.wait()
    start = checkpoint[0]
    first, second = [], []
    for layer in range(2):
        angle = table[slots[start + layer]]
        cosine, sine = jnp.cos(angle), jnp.sin(angle)
        for mode, held in ((0, first), (1, second)):
            re, im = disp[start + layer, mode, 0], disp[start + layer, mode, 1]
            c, s = cosine[mode : mode + 1], sine[mode : mode + 1]
            held.append((re * c - im * s, re * s + im * c))
    va, wa = first
    vb, wb = second
    ua, ub = cmul(wa, va), cmul(wb, vb)
    gh, gl = split(jnp.concatenate([ua[0].T, ua[1].T], axis=0))
    g3[...] = jnp.concatenate([gh, gh, gl], axis=1)
    spread = (
        lax.broadcasted_iota(jnp.int32, (128, 64), 0) // 2 == lax.broadcasted_iota(jnp.int32, (128, 64), 1)
    ).astype(F32)
    parity = (
        lax.broadcasted_iota(jnp.int32, (128, 128), 0) + lax.broadcasted_iota(jnp.int32, (128, 128), 1)
    ) % 2 == 0

    def both(m):
        wide = dot(dot(spread, m, NN, HIGHEST), spread, NT, HIGHEST)
        return jnp.where(parity, wide, 0.0)

    ub, vb, wb = [(both(m[0]), both(m[1])) for m in (ub, vb, wb)]
    left = jnp.concatenate([jnp.concatenate([ub[0], -ub[1]], axis=1), jnp.concatenate([ub[1], ub[0]], axis=1)], axis=0)
    right = jnp.concatenate([jnp.concatenate([ub[0], ub[1]], axis=1), jnp.concatenate([-ub[1], ub[0]], axis=1)], axis=0)
    for m, high, low in ((left, left_hi, left_lo), (right, right_hi, right_lo)):
        for other in range(2):
            high[other], low[other] = split(m.T if other else m)

    loads[2].wait()
    loads[3].wait()
    rho_stage(rin, work, right_hi, right_lo, left_hi, left_lo)
    pack(work, r_send0, True)
    send_near(0, r_send, r_recv, *r_sems, (for_others,))
    turn_over(work, turned)
    pack(turned, r_send1, True)
    send_near(1, r_send, r_recv, *r_sems, (for_others,))

    wait_near(c_recv, c_sems[1])
    flip(c_recv1, t1, c_recv0)
    mode_one(t1, t2, g3, False)
    flip(t2, t1)
    mode_one(t1, t2, g3, True)
    send_some(t2, recv_l, sem.at[8], sem.at[9], 0, 32)
    flip(t2, t3)

    flip(c_recv0, t4, c_recv1, False)
    mode_one(t4, t5, g3, True)
    flip(t5, t4)
    wait_near(r_recv, r_sems[1])
    flip(r_recv1, t5, r_recv0)
    flip(t5, t6)
    send_some(t3, recv_u, sem.at[10], sem.at[11], 0, 19)
    f = gram(t1, t6, 1.0) + gram(t4, t5, -1.0)
    row0, row1 = diagonals(ua, va, wa, (f[:64], f[64:]))

    wait_tiles(recv_l, sem.at[9], TILES - 1)
    unpack(recv_l, work, True)
    m, n = lower_stage(work, rin, right_hi, right_lo, turned)
    j = (
        m[:128, :128] + m[128:, 128:] + n[:128, :128] - n[128:, 128:],
        m[128:, :128] - m[:128, 128:] + n[:128, 128:] + n[128:, :128],
    )
    row2, row3 = diagonals(ub, vb, wb, j, False)
    blank = jnp.zeros((1, 64), F32)
    tile_ref[0] = jnp.concatenate(
        [jnp.concatenate([row0, blank], axis=1), jnp.concatenate([row1, blank], axis=1), row2, row3,
         jnp.zeros((4, 128), F32)], axis=0)

    def spread_out(half, group, held):
        for k, to in enumerate(group):
            pltpu.make_async_remote_copy(
                src_ref=tile_ref.at[half], dst_ref=held.at[k], send_sem=sem.at[12 + half],
                recv_sem=sem.at[14 + half], device_id=to, device_id_type=MESH,
            ).start()

    def add_up(half, held):
        pltpu.make_async_copy(held, held, sem.at[14 + half]).wait()
        value = tile_ref[half]
        for k in range(15):
            value = value + held[k]
        tile_ref[half + 1] = value

    spread_out(0, ring, near)
    send_some(t3, recv_u, sem.at[10], sem.at[11], 19, 32)
    down_stage(turned, left_hi, left_lo, result)
    add_up(0, near)
    spread_out(1, plane, far)

    wait_tiles(recv_u, sem.at[11], TILES - 1)
    unpack(recv_u, work, False)
    upper_stage(work, right_hi, right_lo, left_hi, left_lo, result, out, load)

    add_up(1, far)
    summed = tile_ref[2]
    modes = dot(summed, spread, NN, HIGHEST)
    for layer in range(2):
        grads[layer, 0:1, :] = summed[layer : layer + 1, :64]
        grads[layer, 1:2, :] = modes[2 + layer : 3 + layer, :]
    for half, held in enumerate((near, far)):
        pltpu.make_async_copy(held, held, sem.at[12 + half]).wait()
    wait_near_sent(c_send, c_sems[0])
    wait_near_sent(r_send, r_sems[0])
    wait_tiles(t2, sem.at[8], TILES - 1)
    wait_tiles(t3, sem.at[10], TILES - 1)
    for k in range(4):
        wide = pl.ds(k * 256, 256)
        pltpu.make_async_copy(result.at[:, :, wide], out.at[:, :, wide], load.at[k]).wait()


def per_device(density, costate, phases, displacements, table_slot, checkpoint):
    anywhere = pl.BlockSpec(memory_space=pl.ANY)
    vmem = pl.BlockSpec(memory_space=pltpu.VMEM)
    field = pltpu.VMEM((2, 256, 1024), F32)
    tiles = pltpu.VMEM((8 * TILES, 128), F32)
    spaced = pltpu.VMEM((32 * PITCH, 128), F32)
    matrix = pltpu.VMEM((2, 256, 256), BF16)
    return pl.pallas_call(
        kernel,
        out_shape=(jax.ShapeDtypeStruct(costate.shape, F32), jax.ShapeDtypeStruct((2, 2, LEVELS), F32)),
        in_specs=[anywhere] * 6,
        out_specs=(anywhere, vmem),
        scratch_shapes=[field] * 5
        + [
            pltpu.VMEM(displacements.shape, F32),
            pltpu.VMEM(phases.shape, F32),
            pltpu.SMEM(table_slot.shape, jnp.int32),
            pltpu.SMEM(checkpoint.shape, jnp.int32),
        ]
        + [tiles] * 6 + [spaced] * 10
        + [pltpu.VMEM((128, 192), BF16)]
        + [matrix] * 4
        + [
            pltpu.VMEM((3, 8, 128), F32),
            pltpu.VMEM((15, 8, 128), F32),
            pltpu.VMEM((15, 8, 128), F32),
            pltpu.SemaphoreType.REGULAR,
            pltpu.SemaphoreType.DMA((8,)),
            pltpu.SemaphoreType.DMA((16,)),
        ],
        compiler_params=pltpu.CompilerParams(
            collective_id=0, has_side_effects=True, vmem_limit_bytes=50 * 2**20
        ),
    )(density, costate, phases, displacements, table_slot, checkpoint)


def solution(mesh):
    return jax.shard_map(
        per_device,
        mesh=mesh,
        in_specs=(P(None, "dev", "grp"), P(None, "dev", "grp"), P(), P(), P(), P()),
        out_specs=(P(None, "dev", "grp"), P()),
        check_vma=False,
    )
```
